256 devices in a mesh: dp: 2 (over core), seq: 16 (over y, x), exp: 8 (over z).
Axes of the slice: x: 4, y: 4, z: 8, core: 2. Of those that a mesh axis runs over, the one named last changes fastest.
Arguments:
- query: bfloat16 [16, 2048, 2048], P(('dp', 'exp'), 'seq'), may hold values from -96 to 96
- keys: bfloat16 [16, 2048, 256], P(('dp', 'exp'), 'seq'), may hold values from -6 to 6
- values: bfloat16 [16, 2048, 256], P(('dp', 'exp'), 'seq'), may hold values from -6 to 6
- sinks: float32 [32], replicated, may hold values from -1 to 3
- attn_grad: bfloat16 [16, 2048, 2048], P(('dp', 'exp'), 'seq'), may hold values from -6 to 6
- moe_in: bfloat16 [16, 2048, 2880], P(('dp', 'exp'), 'seq'), may hold values from -6 to 6
- moe_grad: bfloat16 [16, 2048, 2880], P(('dp', 'exp'), 'seq'), may hold values from -6 to 6
- expert_ids: int32 [16, 2048, 4], P(('dp', 'exp'), 'seq'), may hold values from 0 to 127, all different within a row
- route_weights: float32 [16, 2048, 4], P(('dp', 'exp'), 'seq'), may hold values from 0.1 to 0.6
- w_gate_up: bfloat16 [8, 2880, 2, 2880], P('exp', None, None, 'seq'), may hold values from -0.109375 to 0.109375
- w_down: bfloat16 [8, 2880, 2880], P('exp', 'seq'), may hold values from -0.109375 to 0.109375
Outputs:
- attn_out: bfloat16 [16, 2048, 2048], P(('dp', 'exp'), 'seq')
- d_query: bfloat16 [16, 2048, 2048], P(('dp', 'exp'), 'seq')
- d_keys: bfloat16 [16, 2048, 256], P(('dp', 'exp'), 'seq')
- d_values: bfloat16 [16, 2048, 256], P(('dp', 'exp'), 'seq')
- d_sinks: float32 [32], replicated
- moe_out: bfloat16 [16, 2048, 2880], P(('dp', 'exp'), 'seq')
- d_moe_in: bfloat16 [16, 2048, 2880], P(('dp', 'exp'), 'seq')
- d_gate_up: bfloat16 [8, 2880, 2, 2880], P('exp', None, None, 'seq')
- d_down: bfloat16 [8, 2880, 2880], P('exp', 'seq')
The draws below stay inside these ranges and needn't reach their ends.
Inputs may be any that keep to these rules, and one draw needn't show every extreme that they name: `expert_ids`: the 4 ids of a token differ.
All inputs are finite; a program needn't handle non-finite values.
Results may differ from the reference program's by a relative error of at most 0.024.
Values may be sent and summed in bfloat16 or wider, within the bound.
A program may use at most 128 MiB of HBM per device.

```python
import math
import jax
import jax.numpy as jnp
from jax import lax

D = 2880
FF = 2880
HQ = 32
HK = 4
HD = 64
NALL = 128
TOP = 4
TOK_DEV = 128
EXPERTS = 8
LENGTH = 2048
SEQS = 16
CAP = 4
FF_DEV = 180
N_SEQ = 16


def shared_keys(key):
    return jax.random.truncated_normal(key, -6.0, 6.0, (SEQS, LENGTH, HK, HD), jnp.float32)


def draw_keys(key, part):
    base_keys = shared_keys(key)
    return base_keys.reshape(SEQS, LENGTH, HK * HD).astype(jnp.bfloat16)


def draw_query(key, part):
    key = jax.random.fold_in(key, 5)
    first_key = jax.random.fold_in(key, 0)
    fresh = jax.random.truncated_normal(first_key, -6.0, 6.0, (SEQS, LENGTH, HQ, HD), jnp.float32)
    return fresh.reshape(SEQS, LENGTH, HQ * HD).astype(jnp.bfloat16)


def block_scale(rng, extent, cuts, smallest, largest):
    level = 1.0
    for axis_at, shards_of in cuts:
        steps = jax.random.uniform(jax.random.fold_in(jax.random.fold_in(rng, 6), axis_at), (shards_of,), jnp.float32, smallest / len(cuts), largest / len(cuts))
        level = level * jnp.repeat(jnp.exp(steps), extent[axis_at] // shards_of).reshape((-1,) + (1,) * (len(extent) - 1 - axis_at))
    return level


def picks_of(own_key, rows, number_of, top, lift):
    order = jax.random.permutation(jax.random.fold_in(own_key, 1), number_of)
    boost = order
    for power in range(3):
        boost = boost * boost // number_of
    boost = boost * lift // number_of
    chance = jax.random.randint(jax.random.fold_in(own_key, 2), (rows, number_of), 0, 4096) + boost
    sure = jax.random.permutation(jax.random.fold_in(own_key, 3), rows)[jnp.arange(number_of) % rows]
    chance = jnp.where(jnp.arange(rows)[:, None] == sure[None, :], 1 << 14, chance)
    priority = chance * number_of + jnp.arange(number_of)
    return lax.top_k(priority.astype(jnp.int32), top)[1].astype(jnp.int32)


def scatter_about(stream_key, extent, width, reach, cuts=(), kind=jnp.bfloat16):
    factor_of = block_scale(stream_key, extent, cuts, -0.22, 0.18) if cuts else 1.0
    drawn = jax.random.normal(stream_key, extent, jnp.float32) * width * factor_of
    return jnp.minimum(jnp.maximum(drawn, -reach), reach).astype(kind)


def setup_inputs(seed: int = 0) -> dict:
    key_of = jax.random.split(jax.random.key(seed), 12)
    return {
        "query": draw_query(jax.random.fold_in(key_of[11], 71), 0),
        "keys": draw_keys(jax.random.fold_in(key_of[11], 71), 0),
        "values": scatter_about(key_of[2], (SEQS, LENGTH, HK * HD), 1.0, 6.0, ((0, 16), (1, 16))),
        "sinks": jnp.clip(jax.random.uniform(key_of[3], (HQ,), jnp.float32, -1.0, 3.0), -1.0, 3.0),
        "attn_grad": scatter_about(key_of[4], (SEQS, LENGTH, HQ * HD), 1.0, 6.0, ((0, 16), (1, 16))),
        "moe_in": scatter_about(key_of[5], (SEQS, LENGTH, D), 1.0, 6.0, ((0, 16), (1, 16))),
        "moe_grad": scatter_about(key_of[6], (SEQS, LENGTH, D), 1.0, 6.0, ((0, 16), (1, 16))),
        "expert_ids": picks_of(key_of[7], SEQS * LENGTH, NALL, TOP, 512).reshape((SEQS, LENGTH, TOP)),
        "route_weights": jnp.clip(0.1 + 0.5 * jax.random.uniform(key_of[8], (SEQS, LENGTH, TOP), jnp.float32) ** block_scale(key_of[8], (SEQS, LENGTH, TOP), ((0, 16), (1, 16)), -0.2, 0.2), 0.1, 0.6),
        "w_gate_up": scatter_about(key_of[9], (EXPERTS, D, 2, FF), D ** -0.5, 0.109375, ((0, 8), (3, 16))),
        "w_down": scatter_about(key_of[10], (EXPERTS, FF, D), FF ** -0.5, 0.109375, ((0, 8), (1, 16))),
    }


ROPE_BASE = 150000.0
YARN_FACTOR = 32.0
YARN_INITIAL = 4096.0
BETA_FAST = 32.0
BETA_SLOW = 1.0
SWIGLU_ALPHA = 1.702
SCORE_SCALE = 0.125


def rotary_tables(seq_rows):
    half_size = HD // 2
    steps_f = jnp.arange(half_size, dtype=jnp.float32)
    powers = jnp.exp(steps_f * (2.0 * math.log(ROPE_BASE) / HD))
    extrap_freq = 1.0 / powers
    interp_freq = extrap_freq / YARN_FACTOR
    low_end = HD * math.log(YARN_INITIAL / (BETA_FAST * 2.0 * math.pi)) / (2.0 * math.log(ROPE_BASE))
    high_end = HD * math.log(YARN_INITIAL / (BETA_SLOW * 2.0 * math.pi)) / (2.0 * math.log(ROPE_BASE))
    ramp_val = jnp.clip((steps_f - low_end) / (high_end - low_end), 0.0, 1.0)
    inv_freq = interp_freq * ramp_val + extrap_freq * (1.0 - ramp_val)
    concentration = 0.1 * math.log(YARN_FACTOR) + 1.0
    angles = jnp.arange(seq_rows, dtype=jnp.float32)[:, None] * inv_freq[None, :]
    return jnp.cos(angles) * concentration, jnp.sin(angles) * concentration


def rotate(values_in, cos_table, sin_table):
    half_size = values_in.shape[-1] // 2
    first_half = values_in[..., :half_size]
    second_half = values_in[..., half_size:]
    cos_b = cos_table[:, None, :]
    sin_b = sin_table[:, None, :]
    return jnp.concatenate([first_half * cos_b - second_half * sin_b, second_half * cos_b + first_half * sin_b], axis=-1)


def unrotate(values_in, cos_table, sin_table):
    half_size = values_in.shape[-1] // 2
    first_half = values_in[..., :half_size]
    second_half = values_in[..., half_size:]
    cos_b = cos_table[:, None, :]
    sin_b = sin_table[:, None, :]
    return jnp.concatenate([first_half * cos_b + second_half * sin_b, second_half * cos_b - first_half * sin_b], axis=-1)


def rounded(value_in):
    return lax.optimization_barrier(value_in.astype(jnp.bfloat16)).astype(jnp.float32)


def attend_sequence(inputs, sinks, cos_table, sin_table):
    q_seq, k_seq, v_seq, grad_seq = inputs
    group_size = HQ // HK
    local_heads = HQ // N_SEQ
    parts_count = group_size // local_heads
    q_rot = rotate(q_seq.reshape(LENGTH, HQ, HD).astype(jnp.float32), cos_table, sin_table).astype(jnp.bfloat16)
    k_rot = rotate(k_seq.reshape(LENGTH, HK, HD).astype(jnp.float32), cos_table, sin_table).astype(jnp.bfloat16)
    v_all = v_seq.reshape(LENGTH, HK, HD)
    grad_all = grad_seq.reshape(LENGTH, HQ, HD)
    positions = jnp.arange(LENGTH, dtype=jnp.int32)
    causal = positions[:, None] >= positions[None, :]

    def per_head(kv_index):
        q_group = lax.dynamic_slice_in_dim(q_rot, kv_index * group_size, group_size, 1).astype(jnp.float32)
        g_group = lax.dynamic_slice_in_dim(grad_all, kv_index * group_size, group_size, 1).astype(jnp.float32)
        k_head = lax.dynamic_index_in_dim(k_rot, kv_index, 1, keepdims=False).astype(jnp.float32)
        v_head = lax.dynamic_index_in_dim(v_all, kv_index, 1, keepdims=False).astype(jnp.float32)
        sink_group = lax.dynamic_slice_in_dim(sinks, kv_index * group_size, group_size)
        scores = SCORE_SCALE * jnp.einsum('qgd,kd->gqk', q_group, k_head)
        scores = jnp.where(causal[None], scores, -jnp.inf)
        row_top = jnp.maximum(jnp.max(scores, axis=-1), sink_group[:, None])
        expd = jnp.exp(scores - row_top[..., None])
        sink_term = jnp.exp(sink_group[:, None] - row_top)
        total = jnp.sum(expd, axis=-1) + sink_term
        prob_f = expd / total[..., None]
        prob_b = prob_f.astype(jnp.bfloat16).astype(jnp.float32)
        out_heads = jnp.einsum('gqk,kd->qgd', prob_b, v_head).astype(jnp.bfloat16)
        d_prob = jnp.einsum('qgd,kd->gqk', g_group, v_head)
        delta = jnp.sum(prob_f * d_prob, axis=-1)
        d_score = (prob_f * (d_prob - delta[..., None])).astype(jnp.bfloat16).astype(jnp.float32)
        dq_rot = SCORE_SCALE * jnp.einsum('gqk,kd->qgd', d_score, k_head)
        dq_heads = unrotate(dq_rot, cos_table, sin_table).astype(jnp.bfloat16)
        dk_heads = SCORE_SCALE * jnp.einsum('gqk,qgd->gkd', d_score, q_group)
        dk_parts = jnp.sum(dk_heads.reshape(parts_count, local_heads, LENGTH, HD), axis=1)
        dk_parts = unrotate(jnp.transpose(dk_parts, (1, 0, 2)), cos_table, sin_table)
        dk_head = jnp.sum(rounded(dk_parts), axis=1).astype(jnp.bfloat16)
        dv_heads = jnp.einsum('gqk,qgd->gkd', prob_b, g_group)
        dv_parts = jnp.sum(dv_heads.reshape(parts_count, local_heads, LENGTH, HD), axis=1)
        dv_head = jnp.sum(rounded(dv_parts), axis=0).astype(jnp.bfloat16)
        d_sink = -jnp.sum(sink_term / total * delta, axis=1)
        return out_heads, dq_heads, dk_head, dv_head, d_sink

    outs, dqs, dks, dvs, dsinks = lax.map(per_head, jnp.arange(HK, dtype=jnp.int32))
    out_seq = jnp.transpose(outs, (1, 0, 2, 3)).reshape(LENGTH, HQ * HD)
    dq_seq = jnp.transpose(dqs, (1, 0, 2, 3)).reshape(LENGTH, HQ * HD)
    dk_seq = jnp.transpose(dks, (1, 0, 2)).reshape(LENGTH, HK * HD)
    dv_seq = jnp.transpose(dvs, (1, 0, 2)).reshape(LENGTH, HK * HD)
    return out_seq, dq_seq, dk_seq, dv_seq, dsinks.reshape(HQ)


def expert_pass(inputs):
    rows_in, grads_in, gate_up, down_proj = inputs
    flat_rows = rows_in.reshape(-1, D)
    flat_grads = grads_in.reshape(-1, D)
    row_count = flat_rows.shape[0]
    both_proj = jnp.dot(flat_rows, gate_up.reshape(D, 2 * FF), preferred_element_type=jnp.float32).reshape(row_count, 2, FF)
    gate_part = both_proj[:, 0]
    up_part = both_proj[:, 1]
    sigmoid_gate = jax.nn.sigmoid(SWIGLU_ALPHA * gate_part)
    hidden = (gate_part * sigmoid_gate * (up_part + 1.0)).astype(jnp.bfloat16)
    slices_out = jnp.einsum('rsf,sfd->srd', hidden.reshape(row_count, N_SEQ, FF_DEV).astype(jnp.float32), down_proj.reshape(N_SEQ, FF_DEV, D).astype(jnp.float32))
    expert_rows = jnp.sum(rounded(slices_out), axis=0).astype(jnp.bfloat16)
    d_hidden = jnp.dot(flat_grads, down_proj.T, preferred_element_type=jnp.float32)
    d_gate = d_hidden * sigmoid_gate * (up_part + 1.0) * (1.0 + SWIGLU_ALPHA * gate_part * (1.0 - sigmoid_gate))
    d_up = d_hidden * gate_part * sigmoid_gate
    d_both = jnp.stack([d_gate, d_up], axis=1).astype(jnp.bfloat16)
    slices_dx = jnp.einsum('rtsf,dtsf->srd', d_both.reshape(row_count, 2, N_SEQ, FF_DEV).astype(jnp.float32), gate_up.reshape(D, 2, N_SEQ, FF_DEV).astype(jnp.float32))
    dx_rows = jnp.sum(rounded(slices_dx), axis=0).astype(jnp.bfloat16)
    d_gate_up = jnp.dot(flat_rows.T, d_both.reshape(row_count, 2 * FF), preferred_element_type=jnp.float32).reshape(D, 2, FF)
    d_down = jnp.dot(hidden.T, flat_grads, preferred_element_type=jnp.float32)
    shape_rows = rows_in.shape
    return expert_rows.reshape(shape_rows), dx_rows.reshape(shape_rows), d_gate_up.astype(jnp.bfloat16), d_down.astype(jnp.bfloat16)


def reference(query, keys, values, sinks, attn_grad, moe_in, moe_grad, expert_ids, route_weights, w_gate_up, w_down):
    cos_table, sin_table = rotary_tables(LENGTH)
    attend = lambda inputs: attend_sequence(inputs, sinks, cos_table, sin_table)
    attn_out, d_query, d_keys, d_values, sink_parts = lax.map(attend, (query, keys, values, attn_grad))
    d_sinks = jnp.sum(sink_parts, axis=0)

    block_total = SEQS * N_SEQ
    route_ids = expert_ids.reshape(block_total, TOK_DEV, TOP)
    route_share = route_weights.reshape(block_total, TOK_DEV, TOP)
    x_blocks = moe_in.reshape(block_total, TOK_DEV, D)
    g_blocks = moe_grad.reshape(block_total, TOK_DEV, D)
    matches = route_ids[..., None] == jnp.arange(EXPERTS, dtype=jnp.int32)
    hit_table = jnp.any(matches, axis=2)
    token_share = jnp.sum(jnp.where(matches, route_share[..., None], 0.0), axis=2)
    slot_rank = jnp.cumsum(hit_table.astype(jnp.int32), axis=1) - 1
    slot_index = jnp.arange(CAP, dtype=jnp.int32)
    chosen = hit_table[..., None] & (slot_rank[..., None] == slot_index)
    chosen_f = chosen.astype(jnp.float32)
    weighted = jnp.where(chosen, token_share[..., None], 0.0)
    hp = lax.Precision.HIGHEST
    x_rows = jnp.einsum('btec,btd->ebcd', chosen_f, x_blocks.astype(jnp.float32), precision=hp).astype(jnp.bfloat16)
    g_rows = jnp.einsum('btec,btd->ebcd', weighted, g_blocks.astype(jnp.float32), precision=hp).astype(jnp.bfloat16)
    expert_rows, dx_rows, d_gate_up, d_down = lax.map(expert_pass, (x_rows, g_rows, w_gate_up, w_down))
    moe_out = jnp.einsum('btec,ebcd->btd', weighted, expert_rows.astype(jnp.float32), precision=hp).astype(jnp.bfloat16)
    d_moe_in = jnp.einsum('btec,ebcd->btd', chosen_f, dx_rows.astype(jnp.float32), precision=hp).astype(jnp.bfloat16)
    moe_out = moe_out.reshape(SEQS, LENGTH, D)
    d_moe_in = d_moe_in.reshape(SEQS, LENGTH, D)
    return attn_out, d_query, d_keys, d_values, d_sinks, moe_out, d_moe_in, d_gate_up, d_down
```

```python
import math

import jax
import jax.numpy as jnp
from jax import lax
from jax.experimental import pallas as pl
from jax.experimental.pallas import tpu as pltpu
from jax.sharding import PartitionSpec as P

D = 2880
HQ = 32
HK = 4
HD = 64
TOP = 4
CAP = 4
FFD = 180
ROWS = 32

ROPE_BASE = 150000.0
YARN_FACTOR = 32.0
YARN_INITIAL = 4096.0
BETA_FAST = 32.0
BETA_SLOW = 1.0
SWIGLU_ALPHA = 1.702
SCORE_SCALE = 0.125

MESH = pl.DeviceIdType.MESH
F32 = jnp.float32
BF16 = jnp.bfloat16
NT = (((1,), (1,)), ((), ()))
TN = (((0,), (0,)), ((), ()))


def dot(a, b, dims=(((1,), (0,)), ((), ()))):
    return lax.dot_general(a, b, dims, preferred_element_type=F32)


def swap_halves(y, lanes):
    return jnp.where((lanes & 32) == 0, pltpu.roll(y, 96, 1), pltpu.roll(y, 32, 1))


class Comm:
    def __init__(self, send, recv):
        seq = lax.axis_index("seq")
        self.y, self.x = seq // 4, lax.rem(seq, 4)
        self.z = lax.axis_index("exp")
        self.c = lax.axis_index("dp")
        self.send, self.recv, self.used = send, recv, 0
        self.all = []

    def at_x(self, k):
        return {"seq": self.y * 4 + lax.rem(self.x + k, 4)}

    def at_y(self, k):
        return {"seq": lax.rem(self.y + k, 4) * 4 + self.x}

    def at_z(self, k):
        return {"exp": lax.rem(self.z + k, 8)}

    def at_c(self):
        return {"dp": 1 - self.c}

    def copy(self, src, dst, where):
        i = self.used
        self.used += 1
        made = pltpu.make_async_remote_copy(
            src_ref=src,
            dst_ref=dst,
            send_sem=self.send.at[i],
            recv_sem=self.recv.at[i],
            device_id=where,
            device_id_type=MESH,
        )
        self.all.append(made)
        return made


def start(copies):
    for made in copies:
        made.start()


def arrived(copies):
    for made in copies:
        made.wait_recv()


class Gather:
    def __init__(self, comm, buf, x_first):
        self.buf, self.x_first = buf, x_first
        self.rows = buf.shape[2]
        i, j = (comm.y, comm.x) if x_first else (comm.x, comm.y)
        near, far = (comm.at_x, comm.at_y) if x_first else (comm.at_y, comm.at_x)
        h = self.rows // 2
        jl, jr = lax.rem(j + 3, 4), lax.rem(j + 1, 4)
        il, ir = lax.rem(i + 3, 4), lax.rem(i + 1, 4)
        low, high = pl.ds(0, h), pl.ds(h, h)
        b = self.block
        self.steps = [
            [comm.copy(b(i, j), b(i, j), near(1)), comm.copy(b(i, j), b(i, j), near(3))],
            [
                comm.copy(b(i, jl, low), b(i, jl, low), near(1)),
                comm.copy(b(i, jr, high), b(i, jr, high), near(3)),
            ],
            [
                comm.copy(b(i, pl.ds(0, 4)), b(i, pl.ds(0, 4)), far(1)),
                comm.copy(b(i, pl.ds(0, 4)), b(i, pl.ds(0, 4)), far(3)),
            ],
            [
                comm.copy(b(il, pl.ds(0, 2)), b(il, pl.ds(0, 2)), far(1)),
                comm.copy(b(ir, pl.ds(2, 2)), b(ir, pl.ds(2, 2)), far(3)),
            ],
        ]

    def block(self, i, j, rows=None):
        index = (i, j) if self.x_first else (j, i)
        return self.buf.at[index] if rows is None else self.buf.at[index + (rows,)]


class Scatter:
    def __init__(self, comm, buf, y_first, r1, r2, r3, r4):
        self.buf, self.y_first = buf, y_first
        self.rows = buf.shape[2]
        i, j = (comm.y, comm.x) if y_first else (comm.x, comm.y)
        first, second = (comm.at_y, comm.at_x) if y_first else (comm.at_x, comm.at_y)
        self.i, self.j = i, j
        self.r = (r1, r2, r3, r4)
        h = self.rows // 2
        self.i1, self.i2, self.i3 = (lax.rem(i + k, 4) for k in (1, 2, 3))
        self.j1, self.j2, self.j3 = (lax.rem(j + k, 4) for k in (1, 2, 3))
        b = self.block
        self.s1 = [
            comm.copy(b(self.i2, pl.ds(0, 2)), r1.at[0], first(1)),
            comm.copy(b(self.i2, pl.ds(2, 2)), r1.at[1], first(3)),
        ]
        self.s2 = [
            comm.copy(b(self.i1, pl.ds(0, 4)), r2.at[0], first(1)),
            comm.copy(b(self.i3, pl.ds(0, 4)), r2.at[1], first(3)),
        ]
        self.s3 = [
            comm.copy(b(i, self.j2, pl.ds(0, h)), r3.at[0], second(1)),
            comm.copy(b(i, self.j2, pl.ds(h, h)), r3.at[1], second(3)),
        ]
        self.s4 = [
            comm.copy(b(i, self.j1), r4.at[0], second(1)),
            comm.copy(b(i, self.j3), r4.at[1], second(3)),
        ]

    def index(self, i, j):
        return (i, j) if self.y_first else (j, i)

    def block(self, i, j, rows=None):
        index = self.index(i, j)
        return self.buf.at[index] if rows is None else self.buf.at[index + (rows,)]

    def add(self, index, *others):
        total = self.buf[index].astype(F32)
        for other in others:
            total = total + other.astype(F32)
        self.buf[index] = total.astype(BF16)

    def step1(self):
        start(self.s1)

    def step2(self):
        arrived(self.s1)
        r1 = self.r[0]

        def body(k, _):
            self.add(self.index(self.i1, k), r1[0, k])
            self.add(self.index(self.i3, k + 2), r1[1, k])
            return 0

        lax.fori_loop(0, 2, body, 0)
        start(self.s2)

    def step3(self):
        arrived(self.s2)
        r2 = self.r[1]

        def body(k, _):
            self.add(self.index(self.i, k), r2[0, k], r2[1, k])
            return 0

        lax.fori_loop(0, 4, body, 0)
        start(self.s3)

    def step4(self):
        arrived(self.s3)
        r3 = self.r[2]
        h = self.rows // 2
        self.add(self.index(self.i, self.j1) + (pl.ds(0, h),), r3[0])
        self.add(self.index(self.i, self.j3) + (pl.ds(h, h),), r3[1])
        start(self.s4)

    def finish(self):
        arrived(self.s4)
        r4 = self.r[3]
        own = self.buf[self.index(self.i, self.j)].astype(F32)
        return own + r4[0].astype(F32) + r4[1].astype(F32)


def kernel(
    q_ref, k_ref, v_ref, g_ref, x_ref, gy_ref, ids_ref, rw_ref, w_ref, wd_ref, sink_ref, cos_ref, sin_ref,
    out_ref, dq_ref, dk_ref, dv_ref, ds_ref, moe_ref, dx_ref, dw_ref, dwd_ref,
    kb, vb, xb, yb, zs, zr, zs2, zr2, qz, qzt, gz, gzt, kk, vv, kt, vt, e_s, dp_s, m_s, ot, dqt,
    dka, dva, dkp, dvp, wg, wu, hid, dgu, py, px,
    ry1, ry2, ry3, ry4, rx1, rx2, rx3, rx4, rk1, rk2, rk3, rk4, rv1, rv2, rv3, rv4,
    rw, rwd, sx, sy, sz, sc,
    send, recv,
):
    cm = Comm(send, recv)
    me = cm.y * 4 + cm.x

    barrier = pltpu.get_barrier_semaphore()
    partners = [cm.at_x(k) for k in (1, 2, 3)] + [cm.at_y(k) for k in (1, 2, 3)]
    partners += [cm.at_z(k) for k in range(1, 8)] + [cm.at_c()]
    for where in partners:
        pl.semaphore_signal(barrier, inc=1, device_id=where, device_id_type=MESH)

    g_k, g_v = Gather(cm, kb, True), Gather(cm, vb, False)
    g_x, g_y = Gather(cm, xb, True), Gather(cm, yb, False)
    z_out = [
        cm.copy(zs.at[lax.rem(cm.z + k, 8)], zr.at[cm.z], cm.at_z(k)) for k in range(1, 8)
    ]
    z_back = [
        cm.copy(zs2.at[lax.rem(cm.z + k, 8)], zr2.at[cm.z], cm.at_z(k)) for k in range(1, 8)
    ]
    s_k, s_v = Scatter(cm, dka, True, rk1, rk2, rk3, rk4), Scatter(cm, dva, False, rv1, rv2, rv3, rv4)
    s_y, s_x = Scatter(cm, py, True, ry1, ry2, ry3, ry4), Scatter(cm, px, False, rx1, rx2, rx3, rx4)
    dw_out = [cm.copy(dw_ref, rw, cm.at_c()), cm.copy(dwd_ref, rwd, cm.at_c())]
    sink_x = [cm.copy(sx.at[cm.x], sx.at[cm.x], cm.at_x(k)) for k in (1, 2, 3)]
    sink_y = [cm.copy(sy.at[cm.y], sy.at[cm.y], cm.at_y(k)) for k in (1, 2, 3)]
    sink_z = [cm.copy(sz.at[cm.z], sz.at[cm.z], cm.at_z(k)) for k in range(1, 8)]
    sink_c = [cm.copy(sc.at[cm.c], sc.at[cm.c], cm.at_c())]

    lanes = lax.broadcasted_iota(jnp.int32, (128, 128), 1)
    subs = lax.broadcasted_iota(jnp.int32, (128, 128), 0)
    cos_t, sin_t = cos_ref[...], sin_ref[...]

    for t in range(2):
        part = k_ref[:, t * 128 : (t + 1) * 128].astype(F32)
        kb[cm.y, cm.x, :, t * 128 : (t + 1) * 128] = (
            part * cos_t + swap_halves(part, lanes) * sin_t
        ).astype(BF16)
    vb[cm.y, cm.x] = v_ref[...]

    expert, place = subs >> 4, subs & 15
    hit = jnp.zeros((128, 128), F32)
    share = jnp.zeros((128, 128), F32)
    for k in range(TOP):
        match = ids_ref[k : k + 1, :] == expert
        hit = jnp.where(match, 1.0, hit)
        share = share + jnp.where(match, rw_ref[k : k + 1, :], 0.0)
    upper = jnp.where(subs <= lanes, 1.0, 0.0).astype(BF16)
    rank = jnp.where(hit > 0.5, dot(hit.astype(BF16), upper), 0.0).astype(jnp.int32)
    pick_x = (rank == place + 1) & (place < CAP)
    pick_y = (rank == place - CAP + 1) & (place >= CAP) & (place < 2 * CAP)
    sel_x = jnp.where(pick_x, 1.0, 0.0).astype(BF16)
    sel_y = jnp.where(pick_y, 1.0, 0.0).astype(BF16)
    share_y = jnp.sum(jnp.where(pick_y, share, 0.0), axis=1, keepdims=True)
    share_x = jnp.where(pick_x, share, 0.0)
    zs[...] = (
        (dot(sel_x, x_ref[...], NT) + dot(sel_y, gy_ref[...], NT) * share_y)
        .astype(BF16)
        .reshape(8, 16, D)
    )
    zr[cm.z] = zs[cm.z]

    pl.semaphore_wait(barrier, len(partners))

    start(g_k.steps[0] + g_v.steps[0])
    start(z_out)

    def prepare(t, _):
        cut = pl.ds(pl.multiple_of(t * 128, 128), 128)
        part = q_ref[:, cut].astype(F32)
        part = (part * cos_t + swap_halves(part, lanes) * sin_t).astype(BF16).astype(F32)
        part = part * SCORE_SCALE
        grad = g_ref[:, cut].astype(F32)
        for p in range(2):
            rows = slice(p * 128, (p + 1) * 128)
            one = jnp.where((lanes >> 6) == p, part, 0.0)
            qz[t, rows, :] = one.astype(BF16)
            qzt[t, :, rows] = one.T.astype(BF16)
            one = jnp.where((lanes >> 6) == p, grad, 0.0)
            gz[t, rows, :] = one.astype(BF16)
            gzt[t, :, rows] = one.T.astype(BF16)
        return 0

    lax.fori_loop(0, 8, prepare, 0)
    arrived(g_k.steps[0] + g_v.steps[0])
    start(g_k.steps[1] + g_v.steps[1])
    lax.fori_loop(8, 16, prepare, 0)
    arrived(g_k.steps[1] + g_v.steps[1])
    start(g_k.steps[2] + g_v.steps[2])

    r_i = lax.broadcasted_iota(jnp.int32, (FFD, 2 * FFD), 0)
    c_i = lax.broadcasted_iota(jnp.int32, (FFD, 2 * FFD), 1)
    spread_g = jnp.where(c_i == 2 * r_i, 1.0, 0.0).astype(BF16)
    spread_u = jnp.where(c_i == 2 * r_i + 1, 1.0, 0.0).astype(BF16)
    wg[...] = dot(spread_g, w_ref[...]).astype(BF16)
    wu[...] = dot(spread_u, w_ref[...]).astype(BF16)

    def clear(k, _):
        dka[k // 4, lax.rem(k, 4)] = jnp.zeros((128, 256), BF16)
        dva[k // 4, lax.rem(k, 4)] = jnp.zeros((128, 256), BF16)
        return 0

    lax.fori_loop(0, 16, clear, 0)

    arrived(z_out)
    r_i = lax.broadcasted_iota(jnp.int32, (ROWS, 128), 0)
    c_i = lax.broadcasted_iota(jnp.int32, (ROWS, 128), 1)
    home = (r_i >> 2) * 16 + (r_i & 3)
    take_x = jnp.where(c_i == home, 1.0, 0.0).astype(BF16)
    take_y = jnp.where(c_i == home + CAP, 1.0, 0.0).astype(BF16)
    landed = zr[...].reshape(128, D)
    xb[cm.y, cm.x] = dot(take_x, landed).astype(BF16)
    yb[cm.y, cm.x] = dot(take_y, landed).astype(BF16)

    arrived(g_k.steps[2] + g_v.steps[2])
    start(g_k.steps[3] + g_v.steps[3])
    start(g_x.steps[0] + g_y.steps[0])
    arrived(g_k.steps[3] + g_v.steps[3])

    wide = me // 2 + 1
    key_in = lax.broadcasted_iota(jnp.int32, (256, 512), 0)
    query_in = lax.rem(lax.broadcasted_iota(jnp.int32, (256, 512), 1), 128)
    lanes2 = lax.broadcasted_iota(jnp.int32, (256, 128), 1)

    def attend(hh, _):
        group = hh // 2
        lane_cut = pl.ds(pl.multiple_of((group // 2) * 128, 128), 128)
        odd = lax.rem(group, 2)

        @pl.when(lax.rem(hh, 2) == 0)
        def _():
            def spread(j, _):
                rows = pl.ds(lax.rem(j, 2) * 2, 2)
                for source, twice, turned in ((kb, kk, kt), (vb, vv, vt)):
                    part = source[j // 2, rows, :, lane_cut].reshape(256, 128).astype(F32)
                    part = jnp.where((lanes2 >> 6) == odd, part, 0.0)
                    part = part + pltpu.roll(part, 64, 1)
                    twice[j] = part.astype(BF16)
                    turned[j] = part.T[:64].astype(BF16)
                dkp[j] = jnp.zeros((256, 128), F32)
                dvp[j] = jnp.zeros((256, 128), F32)
                return 0

            lax.fori_loop(0, wide, spread, 0)

        sink_row = jnp.concatenate(
            [jnp.full((1, 128), sink_ref[4 * hh + b], F32) for b in range(4)], axis=1
        )
        t0, t1 = 2 * hh, 2 * hh + 1

        def first(j, carry, masked):
            top, z_sum, d_sum = carry
            keys = kk[j]
            s = jnp.concatenate([dot(keys, qzt[t0]), dot(keys, qzt[t1])], axis=1)
            if masked:
                s = jnp.where(key_in + (j * 256 - me * 128) <= query_in, s, -1e30)
            new_top = jnp.maximum(top, jnp.max(s, axis=0, keepdims=True))
            keep = jnp.exp(top - new_top)
            e = jnp.exp(s - new_top)
            vals = vv[j]
            dp = jnp.concatenate([dot(vals, gzt[t0]), dot(vals, gzt[t1])], axis=1)
            e_s[j] = e
            dp_s[j] = dp
            m_s[j] = jnp.broadcast_to(new_top, (8, 512))
            z_sum = z_sum * keep + jnp.sum(e, axis=0, keepdims=True)
            d_sum = d_sum * keep + jnp.sum(e * dp, axis=0, keepdims=True)
            return new_top, z_sum, d_sum

        carry = (sink_row, jnp.ones((1, 512), F32), jnp.zeros((1, 512), F32))
        carry = lax.fori_loop(0, wide - 1, lambda j, c: first(j, c, False), carry)
        top, z_sum, d_sum = first(wide - 1, carry, True)
        inv = 1.0 / z_sum
        delta = d_sum * inv
        sx[cm.x, pl.ds(hh, 1), :] = -jnp.exp(sink_row - top) * inv * delta

        ot[...] = jnp.zeros((64, 512), F32)
        dqt[...] = jnp.zeros((64, 512), F32)

        def second(j, _):
            scale = jnp.exp(m_s[j][0:1] - top) * inv
            p = e_s[j] * scale
            pb = p.astype(BF16)
            ds = (p * (dp_s[j] - delta)).astype(BF16)
            dvp[j] += dot(pb[:, :256], gz[t0]) + dot(pb[:, 256:], gz[t1])
            dkp[j] += dot(ds[:, :256], qz[t0]) + dot(ds[:, 256:], qz[t1])
            ot[...] += dot(vt[j], pb)
            dqt[...] += dot(kt[j], ds)
            return 0

        lax.fori_loop(0, wide, second, 0)

        for i in range(2):
            cut = pl.ds(pl.multiple_of((2 * hh + i) * 128, 128), 128)
            lo, hi = slice(i * 256, i * 256 + 128), slice(i * 256 + 128, i * 256 + 256)
            out_ref[:, cut] = jnp.concatenate([ot[:, lo], ot[:, hi]], axis=0).T.astype(BF16)
            back = jnp.concatenate([dqt[:, lo], dqt[:, hi]], axis=0).T * SCORE_SCALE
            dq_ref[:, cut] = (back * cos_t - swap_halves(back, lanes) * sin_t).astype(BF16)

        @pl.when(lax.rem(hh, 2) == 1)
        def _():
            def collect(j, _):
                rows = pl.ds(lax.rem(j, 2) * 2, 2)
                for source, total in ((dkp, dka), (dvp, dva)):
                    part = source[j]
                    part = part + pltpu.roll(part, 64, 1)
                    part = jnp.where((lanes2 >> 6) == odd, part, 0.0)
                    old = total[j // 2, rows, :, lane_cut].reshape(256, 128).astype(F32)
                    total[j // 2, rows, :, lane_cut] = (old + part).astype(BF16).reshape(2, 128, 128)
                return 0

            lax.fori_loop(0, wide, collect, 0)

        for when, step in ((0, 0), (1, 1), (5, 2)):

            @pl.when(hh == when)
            def _(step=step):
                arrived(g_x.steps[step] + g_y.steps[step])
                start(g_x.steps[step + 1] + g_y.steps[step + 1])

        return 0

    lax.fori_loop(0, 8, attend, 0)

    s_k.step1()
    s_v.step1()
    start(sink_x)

    arrived(g_x.steps[3] + g_y.steps[3])

    def expert_rows(k, _):
        rows = xb[pl.ds(2 * k, 2)].reshape(256, D)
        grads = yb[pl.ds(2 * k, 2)].reshape(256, D)
        gate = dot(rows, wg[...], NT)
        up = dot(rows, wu[...], NT)
        dh = dot(grads, wd_ref[...], NT)
        sig = 1.0 / (1.0 + jnp.exp(-SWIGLU_ALPHA * gate))
        lift = sig * (up + 1.0)
        hid[pl.ds(2 * k, 2)] = (gate * lift).astype(BF16).reshape(2, 4, ROWS, FFD)
        dg = dh * lift * (1.0 + SWIGLU_ALPHA * gate * (1.0 - sig))
        du = dh * gate * sig
        both = dot(dg.astype(BF16), spread_g) + dot(du.astype(BF16), spread_u)
        dgu[pl.ds(2 * k, 2)] = both.astype(BF16).reshape(2, 4, ROWS, 2 * FFD)
        return 0

    lax.fori_loop(0, 2, expert_rows, 0)

    def y_rows(i):
        py[i] = dot(hid[i].reshape(128, FFD), wd_ref[...]).astype(BF16).reshape(4, ROWS, D)

    def x_rows(i):
        px[:, i] = dot(dgu[:, i].reshape(128, 2 * FFD), w_ref[...]).astype(BF16).reshape(4, ROWS, D)

    def chunk(k, _):
        y_rows(lax.rem(cm.y + k, 4))
        x_rows(lax.rem(cm.x + k, 4))
        return 0

    chunk(2, 0)
    s_y.step1()
    s_x.step1()
    s_k.step2()
    s_v.step2()
    lax.fori_loop(0, 2, lambda k, _: chunk(2 * k + 1, 0), 0)
    s_y.step2()
    s_x.step2()
    s_k.step3()
    s_v.step3()
    chunk(0, 0)

    arrived(sink_x)
    sy[cm.y] = ((sx[0] + sx[1]) + sx[2]) + sx[3]
    start(sink_y)

    turned = dgu[...].reshape(512, 2 * FFD).astype(F32).T.astype(BF16)
    turned_h = hid[...].reshape(512, FFD).astype(F32).T.astype(BF16)
    for lo in range(0, D, 512):
        cut = slice(lo, min(lo + 512, D))
        dw_ref[:, cut] = dot(turned, xb[:, :, :, cut].reshape(512, -1)).astype(BF16)
        dwd_ref[:, cut] = dot(turned_h, yb[:, :, :, cut].reshape(512, -1)).astype(BF16)
    start(dw_out)

    s_k.step4()
    s_v.step4()
    s_y.step3()
    s_x.step3()

    arrived(sink_y)
    sz[cm.z] = ((sy[0] + sy[1]) + sy[2]) + sy[3]
    start(sink_z)

    s_y.step4()
    s_x.step4()
    dk = s_k.finish()
    for t in range(2):
        part = dk[:, t * 128 : (t + 1) * 128]
        dk_ref[:, t * 128 : (t + 1) * 128] = (
            part * cos_t - swap_halves(part, lanes) * sin_t
        ).astype(BF16)
    dv_ref[...] = s_v.finish().astype(BF16)

    arrived(sink_z)
    total = sz[0]
    for k in range(1, 8):
        total = total + sz[k]
    sc[cm.c] = total
    start(sink_c)

    y_own = s_y.finish().astype(BF16)
    x_own = s_x.finish().astype(BF16)
    zs2[...] = (dot(take_x, y_own, TN) + dot(take_y, x_own, TN)).astype(BF16).reshape(8, 16, D)
    start(z_back)
    zr2[cm.z] = zs2[cm.z]

    arrived(dw_out)
    for made in dw_out:
        made.wait_send()
    for lo in range(0, D, 512):
        cut = slice(lo, min(lo + 512, D))
        dw_ref[:, cut] = (dw_ref[:, cut].astype(F32) + rw[:, cut].astype(F32)).astype(BF16)
        dwd_ref[:, cut] = (dwd_ref[:, cut].astype(F32) + rwd[:, cut].astype(F32)).astype(BF16)

    arrived(sink_c)
    ds_ref[...] = sc[0] + sc[1]

    arrived(z_back)
    back = zr2[...].reshape(128, D)
    high = share_x.astype(BF16)
    low = (share_x - high.astype(F32)).astype(BF16)
    moe_ref[...] = (dot(back, high, TN) + dot(back, low, TN)).astype(BF16)
    dx_ref[...] = dot(back, sel_y, TN).astype(BF16)

    for made in cm.all:
        if all(made is not other for other in dw_out):
            made.wait_send()


def own_tables(rows):
    steps_f = jnp.arange(HD // 2, dtype=F32)
    extrap_freq = 1.0 / jnp.exp(steps_f * (2.0 * math.log(ROPE_BASE) / HD))
    interp_freq = extrap_freq / YARN_FACTOR
    low_end = HD * math.log(YARN_INITIAL / (BETA_FAST * 2.0 * math.pi)) / (2.0 * math.log(ROPE_BASE))
    high_end = HD * math.log(YARN_INITIAL / (BETA_SLOW * 2.0 * math.pi)) / (2.0 * math.log(ROPE_BASE))
    ramp_val = jnp.clip((steps_f - low_end) / (high_end - low_end), 0.0, 1.0)
    inv_freq = interp_freq * ramp_val + extrap_freq * (1.0 - ramp_val)
    concentration = 0.1 * math.log(YARN_FACTOR) + 1.0
    at = (lax.axis_index("seq") * rows + jnp.arange(rows, dtype=jnp.int32)).astype(F32)
    angles = at[:, None] * jnp.tile(inv_freq, 4)[None, :]
    sign = jnp.where((jnp.arange(128) & 32) == 0, -concentration, concentration)
    return jnp.cos(angles) * concentration, jnp.sin(angles) * sign[None, :]


def body(query, keys, values, sinks, attn_grad, moe_in, moe_grad, expert_ids, route_weights, w_gate_up, w_down):
    rows = query.shape[1]
    cos_t, sin_t = own_tables(rows)
    vmem = pl.BlockSpec(memory_space=pltpu.VMEM)

    def v(*shape, dtype=BF16):
        return pltpu.VMEM(shape, dtype)

    def sums(r, c):
        return [v(2, 2, r, c), v(2, 4, r, c), v(2, r // 2, c), v(2, r, c)]

    scratch = [
        v(4, 4, 128, 256), v(4, 4, 128, 256), v(4, 4, ROWS, D), v(4, 4, ROWS, D),
        v(8, 16, D), v(8, 16, D), v(8, 16, D), v(8, 16, D),
        v(16, 256, 128), v(16, 128, 256), v(16, 256, 128), v(16, 128, 256),
        v(8, 256, 128), v(8, 256, 128), v(8, 64, 256), v(8, 64, 256),
        v(8, 256, 512, dtype=F32), v(8, 256, 512, dtype=F32), v(8, 8, 512, dtype=F32),
        v(64, 512, dtype=F32), v(64, 512, dtype=F32),
        v(4, 4, 128, 256), v(4, 4, 128, 256), v(8, 256, 128, dtype=F32), v(8, 256, 128, dtype=F32),
        v(FFD, D), v(FFD, D), v(4, 4, ROWS, FFD), v(4, 4, ROWS, 2 * FFD),
        v(4, 4, ROWS, D), v(4, 4, ROWS, D),
        *sums(ROWS, D), *sums(ROWS, D), *sums(128, 256), *sums(128, 256),
        v(2 * FFD, D), v(FFD, D),
        v(4, 8, 512, dtype=F32), v(4, 8, 512, dtype=F32), v(8, 8, 512, dtype=F32), v(2, 8, 512, dtype=F32),
        pltpu.SemaphoreType.DMA((96,)),
        pltpu.SemaphoreType.DMA((96,)),
    ]
    sds = jax.ShapeDtypeStruct
    outs = pl.pallas_call(
        kernel,
        out_shape=[
            sds((128, HQ * HD), BF16), sds((128, HQ * HD), BF16),
            sds((128, HK * HD), BF16), sds((128, HK * HD), BF16), sds((8, 512), F32),
            sds((D, 128), BF16), sds((D, 128), BF16), sds((2 * FFD, D), BF16), sds((FFD, D), BF16),
        ],
        in_specs=[vmem] * 10 + [pl.BlockSpec(memory_space=pltpu.SMEM)] + [vmem] * 2,
        out_specs=[vmem] * 9,
        scratch_shapes=scratch,
        compiler_params=pltpu.CompilerParams(
            collective_id=0, has_side_effects=True, vmem_limit_bytes=63 * 1024 * 1024
        ),
        name="layer",
    )(
        query[0], keys[0], values[0], attn_grad[0], moe_in[0].T, moe_grad[0].T,
        expert_ids[0].T, route_weights[0].T,
        jnp.transpose(w_gate_up[0], (2, 1, 0)).reshape(2 * FFD, D), w_down[0], sinks, cos_t, sin_t,
    )
    attn_out, d_query, d_keys, d_values, sink_sum, moe_out, d_moe_in, d_gate_up, d_down = outs
    d_sinks = jnp.sum(sink_sum.reshape(HQ, 128), axis=1)
    d_gate_up = jnp.transpose(d_gate_up.reshape(FFD, 2, D), (2, 1, 0))
    return (
        attn_out[None], d_query[None], d_keys[None], d_values[None], d_sinks,
        moe_out.T[None], d_moe_in.T[None], d_gate_up[None], d_down[None],
    )


def solution(mesh):
    rows = P(("dp", "exp"), "seq", None)
    gate_up, down = P("exp", None, None, "seq"), P("exp", "seq", None)
    return jax.shard_map(
        body,
        mesh=mesh,
        in_specs=(rows, rows, rows, P(), rows, rows, rows, rows, rows, gate_up, down),
        out_specs=(rows, rows, rows, rows, P(), rows, rows, gate_up, down),
        check_vma=False,
    )
```

```python
import math

import jax
import jax.numpy as jnp
import numpy as np
from jax import lax
from jax.experimental import pallas as pl
from jax.experimental.pallas import tpu as pltpu
from jax.sharding import PartitionSpec as P

D = 2880
HQ = 32
HK = 4
HD = 64
TOP = 4
CAP = 4
FFD = 180
ROWS = 32
CUT = 1408
PIECE = D - CUT

ROPE_BASE = 150000.0
YARN_FACTOR = 32.0
YARN_INITIAL = 4096.0
BETA_FAST = 32.0
BETA_SLOW = 1.0
SWIGLU_ALPHA = 1.702
SCORE_SCALE = 0.125
CONCENTRATION = 0.1 * math.log(YARN_FACTOR) + 1.0

MESH = pl.DeviceIdType.MESH
F32 = jnp.float32
BF16 = jnp.bfloat16
NT = (((1,), (1,)), ((), ()))
TN = (((0,), (0,)), ((), ()))


def dot(a, b, dims=(((1,), (0,)), ((), ()))):
    return lax.dot_general(a, b, dims, preferred_element_type=F32)


def swap_halves(y, lanes):
    return jnp.where((lanes & 32) == 0, pltpu.roll(y, 96, 1), pltpu.roll(y, 32, 1))


class Comm:
    def __init__(self, send, recv):
        seq = lax.axis_index("seq")
        self.y, self.x = seq // 4, lax.rem(seq, 4)
        self.z = lax.axis_index("exp")
        self.c = lax.axis_index("dp")
        self.send, self.recv, self.used = send, recv, 0
        self.all = []

    def at_x(self, k):
        return {"seq": self.y * 4 + lax.rem(self.x + k, 4)}

    def at_y(self, k):
        return {"seq": lax.rem(self.y + k, 4) * 4 + self.x}

    def at_z(self, k):
        return {"exp": lax.rem(self.z + k, 8)}

    def at_c(self):
        return {"dp": 1 - self.c}

    def copy(self, src, dst, where):
        i = self.used
        self.used += 1
        made = pltpu.make_async_remote_copy(
            src_ref=src,
            dst_ref=dst,
            send_sem=self.send.at[i],
            recv_sem=self.recv.at[i],
            device_id=where,
            device_id_type=MESH,
        )
        self.all.append(made)
        return made


def start(copies):
    for made in copies:
        made.start()


def arrived(copies):
    for made in copies:
        made.wait_recv()


class Gather:
    def __init__(self, comm, buf, x_first):
        self.buf, self.x_first = buf, x_first
        self.rows = buf.shape[2]
        i, j = (comm.y, comm.x) if x_first else (comm.x, comm.y)
        near, far = (comm.at_x, comm.at_y) if x_first else (comm.at_y, comm.at_x)
        h = self.rows // 2
        jl, jr = lax.rem(j + 3, 4), lax.rem(j + 1, 4)
        il, ir = lax.rem(i + 3, 4), lax.rem(i + 1, 4)
        low, high = pl.ds(0, h), pl.ds(h, h)
        b = self.block
        self.steps = [
            [comm.copy(b(i, j), b(i, j), near(1)), comm.copy(b(i, j), b(i, j), near(3))],
            [
                comm.copy(b(i, jl, low), b(i, jl, low), near(1)),
                comm.copy(b(i, jr, high), b(i, jr, high), near(3)),
            ],
            [
                comm.copy(b(i, pl.ds(0, 4)), b(i, pl.ds(0, 4)), far(1)),
                comm.copy(b(i, pl.ds(0, 4)), b(i, pl.ds(0, 4)), far(3)),
            ],
            [
                comm.copy(b(il, pl.ds(0, 2)), b(il, pl.ds(0, 2)), far(1)),
                comm.copy(b(ir, pl.ds(2, 2)), b(ir, pl.ds(2, 2)), far(3)),
            ],
        ]

    def block(self, i, j, rows=None):
        index = (i, j) if self.x_first else (j, i)
        return self.buf.at[index] if rows is None else self.buf.at[index + (rows,)]


class Scatter:
    def __init__(self, comm, buf, y_first, r1, r2, r3, r4):
        self.buf, self.y_first = buf, y_first
        self.rows = buf.shape[2]
        i, j = (comm.y, comm.x) if y_first else (comm.x, comm.y)
        first, second = (comm.at_y, comm.at_x) if y_first else (comm.at_x, comm.at_y)
        self.i, self.j = i, j
        self.r = (r1, r2, r3, r4)
        h = self.rows // 2
        self.i1, self.i2, self.i3 = (lax.rem(i + k, 4) for k in (1, 2, 3))
        self.j1, self.j2, self.j3 = (lax.rem(j + k, 4) for k in (1, 2, 3))
        b = self.block
        self.s1 = [
            comm.copy(b(self.i2, pl.ds(0, 2)), r1.at[0], first(1)),
            comm.copy(b(self.i2, pl.ds(2, 2)), r1.at[1], first(3)),
        ]
        self.s2 = [
            comm.copy(b(self.i1, pl.ds(0, 4)), r2.at[0], first(1)),
            comm.copy(b(self.i3, pl.ds(0, 4)), r2.at[1], first(3)),
        ]
        self.s3 = [
            comm.copy(b(i, self.j2, pl.ds(0, h)), r3.at[0], second(1)),
            comm.copy(b(i, self.j2, pl.ds(h, h)), r3.at[1], second(3)),
        ]
        self.s4 = [
            comm.copy(b(i, self.j1), r4.at[0], second(1)),
            comm.copy(b(i, self.j3), r4.at[1], second(3)),
        ]

    def index(self, i, j):
        return (i, j) if self.y_first else (j, i)

    def block(self, i, j, rows=None):
        index = self.index(i, j)
        return self.buf.at[index] if rows is None else self.buf.at[index + (rows,)]

    def add(self, index, *others):
        total = self.buf[index].astype(F32)
        for other in others:
            total = total + other.astype(F32)
        self.buf[index] = total.astype(BF16)

    def step1(self):
        start(self.s1)

    def step2(self):
        arrived(self.s1)
        r1 = self.r[0]

        def body(k, _):
            self.add(self.index(self.i1, k), r1[0, k])
            self.add(self.index(self.i3, k + 2), r1[1, k])
            return 0

        lax.fori_loop(0, 2, body, 0)
        start(self.s2)

    def step3(self):
        arrived(self.s2)
        r2 = self.r[1]

        def body(k, _):
            self.add(self.index(self.i, k), r2[0, k], r2[1, k])
            return 0

        lax.fori_loop(0, 4, body, 0)
        start(self.s3)

    def step4(self):
        arrived(self.s3)
        r3 = self.r[2]
        h = self.rows // 2
        self.add(self.index(self.i, self.j1) + (pl.ds(0, h),), r3[0])
        self.add(self.index(self.i, self.j3) + (pl.ds(h, h),), r3[1])
        start(self.s4)

    def finish(self):
        arrived(self.s4)
        r4 = self.r[3]
        own = self.buf[self.index(self.i, self.j)].astype(F32)
        return own + r4[0].astype(F32) + r4[1].astype(F32)


def kernel(
    q_in, k_ref, v_ref, g_in, x_in, gy_in, ids_ref, rw_ref, w_in, wd_in, sink_ref, freq_ref,
    out_hbm, dq_hbm, dk_ref, dv_ref, ds_ref, z_hbm, share_ref, one_ref, dw_hbm, dwd_hbm,
    out_ref, dq_ref, x_ref, gy_ref, w3, wd_ref, wi,
    kb, vb, xb, yb, zs, zr, zs2, zr2, qz, qzt, gz, gzt, kk, vv, kt, vt, e_s, dp_s, m_s, st, ot, dqt,
    dka0, dka1, dva0, dva1, dkp, dvp, wg, wgt, wut, wdt, hid, dgu, py, px,
    ry1, ry2, ry3, ry4, rx1, rx2, rx3, rx4, k01, k02, k03, k04, k11, k12, k13, k14, v01, v02, v03, v04, v11, v12, v13, v14,
    rw, rwd, sx, sy, sz, sc,
    send, recv, local,
):
    cm = Comm(send, recv)
    me = cm.y * 4 + cm.x

    barrier = pltpu.get_barrier_semaphore()
    partners = [cm.at_x(k) for k in (1, 2, 3)] + [cm.at_y(k) for k in (1, 2, 3)]
    partners += [cm.at_z(k) for k in range(1, 8)] + [cm.at_c()]
    for where in partners:
        pl.semaphore_signal(barrier, inc=1, device_id=where, device_id_type=MESH)

    pairs = ((x_in, x_ref), (gy_in, gy_ref), (q_in, out_ref), (g_in, dq_ref), (w_in, w3), (wd_in, wd_ref))
    loads = [pltpu.make_async_copy(a, b, local.at[i]) for i, (a, b) in enumerate(pairs)]
    for load in loads:
        load.start()
    pairs = (
        (out_ref, out_hbm), (dq_ref, dq_hbm), (zr2, z_hbm), (w3, dw_hbm), (wd_ref, dwd_hbm),
    )
    stores = [pltpu.make_async_copy(a, b, local.at[6 + i]) for i, (a, b) in enumerate(pairs)]
    out_store, dq_store, z_store, dw_store, dwd_store = stores

    g_k, g_v = Gather(cm, kb, True), Gather(cm, vb, False)
    g_x, g_y = Gather(cm, xb, True), Gather(cm, yb, False)
    z_out = [
        cm.copy(zs.at[lax.rem(cm.z + k, 8)], zr.at[cm.z], cm.at_z(k)) for k in range(1, 8)
    ]
    z_back = [
        cm.copy(zs2.at[lax.rem(cm.z + k, 8)], zr2.at[cm.z], cm.at_z(k)) for k in range(1, 8)
    ]
    s_kv = [
        (Scatter(cm, dka0, True, k01, k02, k03, k04), Scatter(cm, dva0, False, v01, v02, v03, v04)),
        (Scatter(cm, dka1, True, k11, k12, k13, k14), Scatter(cm, dva1, False, v11, v12, v13, v14)),
    ]
    s_y, s_x = Scatter(cm, py, True, ry1, ry2, ry3, ry4), Scatter(cm, px, False, rx1, rx2, rx3, rx4)
    dw_out = [cm.copy(wi, rw, cm.at_c()), cm.copy(wg, rwd, cm.at_c())]
    sink_x = [cm.copy(sx.at[cm.x], sx.at[cm.x], cm.at_x(k)) for k in (1, 2, 3)]
    sink_y = [cm.copy(sy.at[cm.y], sy.at[cm.y], cm.at_y(k)) for k in (1, 2, 3)]
    sink_z = [cm.copy(sz.at[cm.z], sz.at[cm.z], cm.at_z(k)) for k in range(1, 8)]
    sink_c = [cm.copy(sc.at[cm.c], sc.at[cm.c], cm.at_c())]

    lanes = lax.broadcasted_iota(jnp.int32, (128, 128), 1)
    subs = lax.broadcasted_iota(jnp.int32, (128, 128), 0)
    angles = (subs + me * 128).astype(F32) * freq_ref[...]
    cos_t = jnp.cos(angles) * CONCENTRATION
    sin_t = jnp.sin(angles) * jnp.where((lanes & 32) == 0, -CONCENTRATION, CONCENTRATION)

    for t in range(2):
        part = k_ref[:, t * 128 : (t + 1) * 128].astype(F32)
        kb[cm.y, cm.x, :, t * 128 : (t + 1) * 128] = (
            part * cos_t + swap_halves(part, lanes) * sin_t
        ).astype(BF16)
    vb[cm.y, cm.x] = v_ref[...]

    expert, place = subs >> 4, subs & 7
    hit = jnp.zeros((128, 128), F32)
    share = jnp.zeros((128, 128), F32)
    for k in range(TOP):
        match = ids_ref[k : k + 1, :] == expert
        hit = jnp.where(match, 1.0, hit)
        share = share + jnp.where(match, rw_ref[k : k + 1, :], 0.0)
    upper = jnp.where(subs <= lanes, 1.0, 0.0).astype(BF16)
    rank = jnp.where(hit > 0.5, dot(hit.astype(BF16), upper), 0.0).astype(jnp.int32)
    pick_x = (rank == place + 1) & (place < CAP)
    pick_y = (rank == place - CAP + 1) & (place >= CAP)
    one_x = jnp.where(pick_x, 1.0, 0.0)
    one_y = jnp.where(pick_y, 1.0, 0.0)
    share_y = jnp.sum(jnp.where(pick_y, share, 0.0), axis=1, keepdims=True)
    share_ref[...] = jnp.where(pick_x, share, 0.0)
    one_ref[...] = one_y
    is_low = (subs & 8) == 0

    def parts(table):
        low = jnp.where(is_low, table, 0.0)
        return low.astype(BF16), (table - low).astype(BF16)

    pl.semaphore_wait(barrier, len(partners))
    start(g_k.steps[0] + g_v.steps[0])

    for load in loads[:2]:
        load.wait()
    (x_low, x_high), (y_low, y_high) = parts(one_x), parts(one_y)
    picked = dot(x_low, x_ref[:PIECE], NT) + dot(x_high, x_ref[CUT:], NT)
    picked += (dot(y_low, gy_ref[:PIECE], NT) + dot(y_high, gy_ref[CUT:], NT)) * share_y
    zs[...] = picked.astype(BF16).reshape(8, 16, PIECE)
    start(z_out)
    zr[cm.z] = zs[cm.z]

    def prepare(t, _):
        cut = pl.ds(pl.multiple_of(t * 128, 128), 128)
        part = out_ref[:, cut].astype(F32)
        part = (part * cos_t + swap_halves(part, lanes) * sin_t).astype(BF16).astype(F32)
        part = part * SCORE_SCALE
        grad = dq_ref[:, cut].astype(F32)
        for p in range(2):
            rows = slice(p * 128, (p + 1) * 128)
            one = jnp.where((lanes >> 6) == p, part, 0.0)
            qz[t, rows, :] = one.astype(BF16)
            qzt[t, :, rows] = one.T.astype(BF16)
            one = jnp.where((lanes >> 6) == p, grad, 0.0)
            gz[t, rows, :] = one.astype(BF16)
            gzt[t, :, rows] = one.T.astype(BF16)
        return 0

    for load in loads[2:4]:
        load.wait()
    arrived(g_k.steps[0] + g_v.steps[0])
    start(g_k.steps[1] + g_v.steps[1])
    lax.fori_loop(0, 8, prepare, 0)
    arrived(g_k.steps[1] + g_v.steps[1])
    start(g_k.steps[2] + g_v.steps[2])
    lax.fori_loop(8, 16, prepare, 0)

    arrived(z_out)
    r_i = lax.broadcasted_iota(jnp.int32, (ROWS, 128), 0)
    c_i = lax.broadcasted_iota(jnp.int32, (ROWS, 128), 1)
    home = (r_i >> 2) * 16 + (r_i & 3)
    takes = [jnp.where(c_i == home + k, 1.0, 0.0).astype(BF16) for k in (0, 4, 8, 12)]
    landed = zr[...].reshape(128, PIECE)
    for own, low, high in ((xb, takes[0], takes[2]), (yb, takes[1], takes[3])):
        own[cm.y, cm.x] = jnp.concatenate(
            [dot(low, landed[:, :CUT]).astype(BF16), dot(high, landed).astype(BF16)], axis=1
        )

    arrived(g_k.steps[2] + g_v.steps[2])
    start(g_k.steps[3] + g_v.steps[3])
    start(g_x.steps[0] + g_y.steps[0])

    for load in loads[4:]:
        load.wait()
    wi[...] = w3[...].reshape(2 * FFD, D)
    r_i = lax.broadcasted_iota(jnp.int32, (FFD, 2 * FFD), 0)
    c_i = lax.broadcasted_iota(jnp.int32, (FFD, 2 * FFD), 1)
    spread_g = jnp.where(c_i == 2 * r_i, 1.0, 0.0).astype(BF16)
    spread_u = jnp.where(c_i == 2 * r_i + 1, 1.0, 0.0).astype(BF16)
    wgt[...] = dot(spread_g, wi[...]).T.astype(BF16)
    wut[...] = dot(spread_u, wi[...]).T.astype(BF16)
    wdt[...] = wd_ref[...].astype(F32).T.astype(BF16)

    def clear(k, _):
        for total in (dka0, dka1, dva0, dva1):
            total[k // 4, lax.rem(k, 4)] = jnp.zeros((128, 128), BF16)
        return 0

    lax.fori_loop(0, 16, clear, 0)
    arrived(g_k.steps[3] + g_v.steps[3])

    wide = me // 2 + 1
    key_in = lax.broadcasted_iota(jnp.int32, (256, 512), 0)
    query_in = lax.rem(lax.broadcasted_iota(jnp.int32, (256, 512), 1), 128)
    lanes2 = lax.broadcasted_iota(jnp.int32, (256, 128), 1)

    def lane_cut(group):
        return pl.ds(pl.multiple_of((group // 2) * 128, 128), 128), lax.rem(group, 2)

    def spread_keys(group):
        cut, odd = lane_cut(group)

        def spread(j, _):
            rows = pl.ds(lax.rem(j, 2) * 2, 2)
            for source, twice, turned in ((kb, kk, kt), (vb, vv, vt)):
                part = source[j // 2, rows, :, cut].reshape(256, 128).astype(F32)
                part = jnp.where((lanes2 >> 6) == odd, part, 0.0)
                part = part + pltpu.roll(part, 64, 1)
                twice[j] = part.astype(BF16)
                turned[j] = part.T[:64].astype(BF16)
            dkp[j] = jnp.zeros((256, 128), F32)
            dvp[j] = jnp.zeros((256, 128), F32)
            return 0

        lax.fori_loop(0, wide, spread, 0)

    def collect_keys(group, half):
        odd = lax.rem(group, 2)
        totals = ((dkp, (dka0, dka1)[half]), (dvp, (dva0, dva1)[half]))

        def collect(j, _):
            rows = pl.ds(lax.rem(j, 2) * 2, 2)
            for source, total in totals:
                part = source[j]
                part = part + pltpu.roll(part, 64, 1)
                part = jnp.where((lanes2 >> 6) == odd, part, 0.0)
                old = total[j // 2, rows].reshape(256, 128).astype(F32)
                total[j // 2, rows] = (old + part).astype(BF16).reshape(2, 128, 128)
            return 0

        lax.fori_loop(0, wide, collect, 0)

    def scores(hh):
        t0, t1 = 2 * hh, 2 * hh + 1
        sink_row = jnp.concatenate(
            [jnp.full((1, 128), sink_ref[4 * hh + b], F32) for b in range(4)], axis=1
        )

        def first(j, carry, masked):
            top, z_sum, d_sum = carry
            keys = kk[j]
            s = jnp.concatenate([dot(keys, qzt[t0]), dot(keys, qzt[t1])], axis=1)
            if masked:
                s = jnp.where(key_in + (j * 256 - me * 128) <= query_in, s, -1e30)
            new_top = jnp.maximum(top, jnp.max(s, axis=0, keepdims=True))
            keep = jnp.exp(top - new_top)
            e = jnp.exp(s - new_top)
            vals = vv[j]
            dp = jnp.concatenate([dot(vals, gzt[t0]), dot(vals, gzt[t1])], axis=1)
            e_s[j] = e
            dp_s[j] = dp
            m_s[j] = jnp.broadcast_to(new_top, (8, 512))
            z_sum = z_sum * keep + jnp.sum(e, axis=0, keepdims=True)
            d_sum = d_sum * keep + jnp.sum(e * dp, axis=0, keepdims=True)
            return new_top, z_sum, d_sum

        carry = (sink_row, jnp.ones((1, 512), F32), jnp.zeros((1, 512), F32))
        carry = lax.fori_loop(0, wide - 1, lambda j, c: first(j, c, False), carry)
        top, z_sum, d_sum = first(wide - 1, carry, True)
        inv = 1.0 / z_sum
        delta = d_sum * inv
        sx[cm.x, pl.ds(hh, 1), :] = -jnp.exp(sink_row - top) * inv * delta
        for k, row in enumerate((top, inv, delta)):
            st[k] = jnp.broadcast_to(row, (8, 512))

    def gradients(hh):
        t0 = 2 * hh
        top, inv, delta = (st[k][0:1] for k in range(3))
        ot[...] = jnp.zeros((64, 512), F32)
        dqt[...] = jnp.zeros((64, 512), F32)

        def second(j, _):
            scale = jnp.exp(m_s[j][0:1] - top) * inv
            p = e_s[j] * scale
            pb = p.astype(BF16)
            ds = (p * (dp_s[j] - delta)).astype(BF16)
            dvp[j] += dot(pb, gz[pl.ds(t0, 2)].reshape(512, 128))
            dkp[j] += dot(ds, qz[pl.ds(t0, 2)].reshape(512, 128))
            ot[...] += dot(vt[j], pb)
            dqt[...] += dot(kt[j], ds)
            return 0

        lax.fori_loop(0, wide, second, 0)

        for i in range(2):
            cut = pl.ds(pl.multiple_of((2 * hh + i) * 128, 128), 128)
            lo, hi = slice(i * 256, i * 256 + 128), slice(i * 256 + 128, i * 256 + 256)
            out_ref[:, cut] = jnp.concatenate([ot[:, lo], ot[:, hi]], axis=0).T.astype(BF16)
            back = jnp.concatenate([dqt[:, lo], dqt[:, hi]], axis=0).T * SCORE_SCALE
            dq_ref[:, cut] = (back * cos_t - swap_halves(back, lanes) * sin_t).astype(BF16)

    def attend(u, half, hooks):
        hh = u // 2
        pl.when(lax.rem(u, 4) == 0)(lambda: spread_keys(hh // 2))
        pl.when(lax.rem(u, 2) == 0)(lambda: scores(hh))
        pl.when(lax.rem(u, 2) == 1)(lambda: gradients(hh))
        pl.when(lax.rem(u, 4) == 3)(lambda: collect_keys(hh // 2, half))
        for when, hook in hooks:
            pl.when(u == when)(hook)
        return 0

    def gather_on(step):
        def hook():
            arrived(g_x.steps[step] + g_y.steps[step])
            start(g_x.steps[step + 1] + g_y.steps[step + 1])

        return hook

    hooks = ((0, gather_on(0)), (1, gather_on(1)), (5, gather_on(2)))
    lax.fori_loop(0, 8, lambda u, _: attend(u, 0, hooks), 0)

    def kv_on(half, name):
        getattr(s_kv[half][0], name)()
        getattr(s_kv[half][1], name)()

    kv_on(0, "step1")

    arrived(g_x.steps[3] + g_y.steps[3])

    def expert_rows(k, _):
        rows = xb[pl.ds(2 * k, 2)].reshape(256, D)
        grads = yb[pl.ds(2 * k, 2)].reshape(256, D)
        gate = dot(rows, wgt[...])
        up = dot(rows, wut[...])
        dh = dot(grads, wdt[...])
        sig = 1.0 / (1.0 + jnp.exp(-SWIGLU_ALPHA * gate))
        lift = sig * (up + 1.0)
        hid[pl.ds(2 * k, 2)] = (gate * lift).astype(BF16).reshape(2, 4, ROWS, FFD)
        dg = dh * lift * (1.0 + SWIGLU_ALPHA * gate * (1.0 - sig))
        du = dh * gate * sig
        both = dot(dg.astype(BF16), spread_g) + dot(du.astype(BF16), spread_u)
        dgu[pl.ds(2 * k, 2)] = both.astype(BF16).reshape(2, 4, ROWS, 2 * FFD)
        return 0

    lax.fori_loop(0, 2, expert_rows, 0)

    def y_rows(i):
        py[i] = dot(hid[i].reshape(128, FFD), wd_ref[...]).astype(BF16).reshape(4, ROWS, D)

    def x_rows(i):
        px[:, i] = dot(dgu[:, i].reshape(128, 2 * FFD), wi[...]).astype(BF16).reshape(4, ROWS, D)

    def chunk(k, _):
        y_rows(lax.rem(cm.y + k, 4))
        x_rows(lax.rem(cm.x + k, 4))
        return 0

    kv_on(0, "step2")
    chunk(2, 0)
    s_y.step1()
    s_x.step1()
    lax.fori_loop(0, 2, lambda k, _: chunk(2 * k + 1, 0), 0)
    chunk(0, 0)

    turned = dgu[...].reshape(512, 2 * FFD).astype(F32).T.astype(BF16)
    turned_h = hid[...].reshape(512, FFD).astype(F32).T.astype(BF16)
    for lo in range(0, D, 512):
        cut = slice(lo, min(lo + 512, D))
        wi[:, cut] = dot(turned, xb[:, :, :, cut].reshape(512, -1)).astype(BF16)
        wg[:, cut] = dot(turned_h, yb[:, :, :, cut].reshape(512, -1)).astype(BF16)
    start(dw_out)
    kv_on(0, "step3")

    def both_sums(name):
        def hook():
            getattr(s_y, name)()
            getattr(s_x, name)()

        return hook

    def send_back():
        y_own = s_y.finish().astype(BF16)
        x_own = s_x.finish().astype(BF16)
        returned = dot(takes[0], y_own[:, :PIECE], TN) + dot(takes[1], x_own[:, :PIECE], TN)
        returned += dot(takes[2], y_own[:, CUT:], TN) + dot(takes[3], x_own[:, CUT:], TN)
        zs2[...] = returned.astype(BF16).reshape(8, 16, PIECE)
        start(z_back)
        zr2[cm.z] = zs2[cm.z]

    hooks = (
        (8, both_sums("step2")), (8, lambda: kv_on(0, "step4")), (12, both_sums("step3")), (13, both_sums("step4")),
        (14, lambda: start(sink_x)),
    )
    lax.fori_loop(8, 16, lambda u, _: attend(u, 1, hooks), 0)

    kv_on(1, "step1")
    send_back()
    out_store.start()
    dq_store.start()
    arrived(sink_x)
    sy[cm.y] = ((sx[0] + sx[1]) + sx[2]) + sx[3]
    start(sink_y)
    kv_on(1, "step2")
    arrived(sink_y)
    sz[cm.z] = ((sy[0] + sy[1]) + sy[2]) + sy[3]
    start(sink_z)

    arrived(dw_out)
    for lo in range(0, D, 512):
        cut = slice(lo, min(lo + 512, D))
        total = wi[:, cut].astype(F32) + rw[:, cut].astype(F32)
        w3[:, :, cut] = total.astype(BF16).reshape(FFD, 2, -1)
        wd_ref[:, cut] = (wg[:, cut].astype(F32) + rwd[:, cut].astype(F32)).astype(BF16)
    dw_store.start()
    dwd_store.start()

    kv_on(1, "step3")
    arrived(sink_z)
    total = sz[0]
    for k in range(1, 8):
        total = total + sz[k]
    sc[cm.c] = total
    start(sink_c)
    kv_on(1, "step4")

    for t, (k_part, v_part) in enumerate(s_kv):
        cut = slice(t * 128, (t + 1) * 128)
        part = k_part.finish()
        dk_ref[:, cut] = (part * cos_t - swap_halves(part, lanes) * sin_t).astype(BF16)
        dv_ref[:, cut] = v_part.finish().astype(BF16)

    arrived(sink_c)
    total = sc[0] + sc[1]
    row8 = lax.broadcasted_iota(jnp.int32, (8, HQ), 0)
    lane8 = lax.broadcasted_iota(jnp.int32, (8, HQ), 1)
    sums = jnp.zeros((8, HQ), F32)
    for b in range(4):
        part = jnp.sum(total[:, b * 128 : (b + 1) * 128], axis=1, keepdims=True)
        sums = sums + jnp.where(lane8 == 4 * row8 + b, part, 0.0)
    ds_ref[...] = jnp.sum(sums, axis=0, keepdims=True)

    arrived(z_back)
    z_store.start()
    for made in cm.all:
        made.wait_send()
    for store in stores:
        store.wait()


def finish(*refs):
    (z_ref, share_ref, one_ref), refs = refs[:3], refs[3:]
    sources, (moe_hbm, dx_hbm), results, held = refs[:7], refs[7:9], refs[9:16], refs[16:23]
    moe, dx, sems = refs[23:]
    loads = [pltpu.make_async_copy(sources[i], held[i], sems.at[i]) for i in range(7)]
    stores = [pltpu.make_async_copy(held[i], results[i], sems.at[7 + i]) for i in range(7)]
    last = [pltpu.make_async_copy(moe, moe_hbm, sems.at[14]), pltpu.make_async_copy(dx, dx_hbm, sems.at[15])]
    for load in loads:
        load.start()

    low_rows = (lax.broadcasted_iota(jnp.int32, (128, 128), 0) & 8) == 0
    share = share_ref[...]
    top = share.astype(BF16).astype(F32)
    tables = []
    for table in (top, share - top, one_ref[...]):
        low = jnp.where(low_rows, table, 0.0)
        tables.append((low.astype(BF16), (table - low).astype(BF16)))
    where = ((0, 768, 0, 0), (768, 640, 768, 0), (0, 768, CUT, 1), (768, 704, CUT + 768, 1))
    for i in range(7):
        loads[i].wait()
        stores[i].start()
        if i < 4:
            lane, n, at, high = where[i]
            back = z_ref[:, :, lane : lane + n].reshape(128, n)
            moe[at : at + n] = (dot(back, tables[0][high], TN) + dot(back, tables[1][high], TN)).astype(BF16)
            dx[at : at + n] = dot(back, tables[2][high], TN).astype(BF16)
    for made in last:
        made.start()
    for made in stores + last:
        made.wait()


def frequencies():
    steps_f = np.arange(HD // 2, dtype=np.float32)
    extrap_freq = np.float32(1.0) / np.exp(steps_f * np.float32(2.0 * math.log(ROPE_BASE) / HD))
    interp_freq = extrap_freq / np.float32(YARN_FACTOR)
    low_end = HD * math.log(YARN_INITIAL / (BETA_FAST * 2.0 * math.pi)) / (2.0 * math.log(ROPE_BASE))
    high_end = HD * math.log(YARN_INITIAL / (BETA_SLOW * 2.0 * math.pi)) / (2.0 * math.log(ROPE_BASE))
    ramp_val = np.clip((steps_f - np.float32(low_end)) / np.float32(high_end - low_end), 0.0, 1.0)
    inv_freq = interp_freq * ramp_val + extrap_freq * (np.float32(1.0) - ramp_val)
    return jnp.asarray(np.tile(inv_freq, 4)[None, :], F32)


def body(query, keys, values, sinks, attn_grad, moe_in, moe_grad, expert_ids, route_weights, w_gate_up, w_down):
    rows = query.shape[1]
    vmem = pl.BlockSpec(memory_space=pltpu.VMEM)

    def v(*shape, dtype=BF16):
        return pltpu.VMEM(shape, dtype)

    def sums(r, c):
        return [v(2, 2, r, c), v(2, 4, r, c), v(2, r // 2, c), v(2, r, c)]

    scratch = [
        v(rows, HQ * HD), v(rows, HQ * HD), v(D, rows), v(D, rows), v(FFD, 2, D), v(FFD, D), v(2 * FFD, D),
        v(4, 4, 128, 256), v(4, 4, 128, 256), v(4, 4, ROWS, D), v(4, 4, ROWS, D),
        v(8, 16, PIECE), v(8, 16, PIECE), v(8, 16, PIECE), v(8, 16, PIECE),
        v(16, 256, 128), v(16, 128, 256), v(16, 256, 128), v(16, 128, 256),
        v(8, 256, 128), v(8, 256, 128), v(8, 64, 256), v(8, 64, 256),
        v(8, 256, 512, dtype=F32), v(8, 256, 512, dtype=F32), v(8, 8, 512, dtype=F32),
        v(3, 8, 512, dtype=F32), v(64, 512, dtype=F32), v(64, 512, dtype=F32),
        *[v(4, 4, 128, 128)] * 4, v(8, 256, 128, dtype=F32), v(8, 256, 128, dtype=F32),
        v(FFD, D), *[v(D, FFD)] * 3, v(4, 4, ROWS, FFD), v(4, 4, ROWS, 2 * FFD),
        v(4, 4, ROWS, D), v(4, 4, ROWS, D),
        *sums(ROWS, D), *sums(ROWS, D), *sums(128, 128) * 4,
        v(2 * FFD, D), v(FFD, D),
        v(4, 8, 512, dtype=F32), v(4, 8, 512, dtype=F32), v(8, 8, 512, dtype=F32), v(2, 8, 512, dtype=F32),
        pltpu.SemaphoreType.DMA((112,)),
        pltpu.SemaphoreType.DMA((112,)),
        pltpu.SemaphoreType.DMA((12,)),
    ]
    sds = jax.ShapeDtypeStruct
    attn = [
        sds((rows, HQ * HD), BF16), sds((rows, HQ * HD), BF16),
        sds((rows, HK * HD), BF16), sds((rows, HK * HD), BF16), sds((1, HQ), F32),
    ]
    weights = [sds((FFD, 2, D), BF16), sds((FFD, D), BF16)]
    back = [sds((8, 16, PIECE), BF16)] + [sds((128, rows), F32)] * 2
    token = [sds((D, rows), BF16)] * 2
    hbm = pl.BlockSpec(memory_space=pl.ANY)
    smem = pl.BlockSpec(memory_space=pltpu.SMEM)
    outs = pl.pallas_call(
        kernel,
        out_shape=attn + back + weights,
        in_specs=[hbm, vmem, vmem, hbm, hbm, hbm, vmem, vmem, hbm, hbm, smem, vmem],
        out_specs=[hbm, hbm, vmem, vmem, vmem, hbm, vmem, vmem, hbm, hbm],
        scratch_shapes=scratch,
        compiler_params=pltpu.CompilerParams(
            collective_id=0, has_side_effects=True, vmem_limit_bytes=63 * 1024 * 1024
        ),
        name="layer",
    )(
        query[0], keys[0], values[0], attn_grad[0], moe_in[0].T, moe_grad[0].T,
        expert_ids[0].T, route_weights[0].T,
        jnp.transpose(w_gate_up[0], (2, 1, 0)), w_down[0], sinks, frequencies(),
    )
    outs = pl.pallas_call(
        finish,
        out_shape=token + attn + weights,
        in_specs=[vmem] * 3 + [hbm] * 7,
        out_specs=[hbm] * 9,
        scratch_shapes=[v(*one.shape, dtype=one.dtype) for one in attn + weights + token]
        + [pltpu.SemaphoreType.DMA((16,))],
        compiler_params=pltpu.CompilerParams(vmem_limit_bytes=63 * 1024 * 1024),
        name="finish",
    )(*outs[5:8], *outs[:5], *outs[8:])
    moe_out, d_moe_in, attn_out, d_query, d_keys, d_values, d_sinks, d_gate_up, d_down = outs
    return (
        attn_out[None], d_query[None], d_keys[None], d_values[None], d_sinks.reshape(HQ),
        moe_out.T[None], d_moe_in.T[None], jnp.transpose(d_gate_up, (2, 1, 0))[None], d_down[None],
    )


def solution(mesh):
    rows = P(("dp", "exp"), "seq", None)
    gate_up, down = P("exp", None, None, "seq"), P("exp", "seq", None)
    return jax.shard_map(
        body,
        mesh=mesh,
        in_specs=(rows, rows, rows, P(), rows, rows, rows, rows, rows, gate_up, down),
        out_specs=(rows, rows, rows, rows, P(), rows, rows, gate_up, down),
        check_vma=False,
    )
```

```python
import math

import jax
import jax.numpy as jnp
import numpy as np
from jax import lax
from jax.experimental import pallas as pl
from jax.experimental.pallas import tpu as pltpu
from jax.sharding import PartitionSpec as P

D = 2880
HQ = 32
HK = 4
HD = 64
TOP = 4
CAP = 4
FFD = 180
ROWS = 32
CUT = 1408
PIECE = D - CUT

ROPE_BASE = 150000.0
YARN_FACTOR = 32.0
YARN_INITIAL = 4096.0
BETA_FAST = 32.0
BETA_SLOW = 1.0
SWIGLU_ALPHA = 1.702
SCORE_SCALE = 0.125
CONCENTRATION = 0.1 * math.log(YARN_FACTOR) + 1.0

MESH = pl.DeviceIdType.MESH
F32 = jnp.float32
BF16 = jnp.bfloat16
NT = (((1,), (1,)), ((), ()))
TN = (((0,), (0,)), ((), ()))


def dot(a, b, dims=(((1,), (0,)), ((), ()))):
    return lax.dot_general(a, b, dims, preferred_element_type=F32)


def swap_halves(y, lanes):
    return jnp.where((lanes & 32) == 0, pltpu.roll(y, 96, 1), pltpu.roll(y, 32, 1))


class Comm:
    def __init__(self, send, recv):
        seq = lax.axis_index("seq")
        self.y, self.x = seq // 4, lax.rem(seq, 4)
        self.z = lax.axis_index("exp")
        self.c = lax.axis_index("dp")
        self.send, self.recv, self.used = send, recv, 0
        self.all = []

    def at_x(self, k):
        return {"seq": self.y * 4 + lax.rem(self.x + k, 4)}

    def at_y(self, k):
        return {"seq": lax.rem(self.y + k, 4) * 4 + self.x}

    def at_z(self, k):
        return {"exp": lax.rem(self.z + k, 8)}

    def at_c(self):
        return {"dp": 1 - self.c}

    def copy(self, src, dst, where):
        i = self.used
        self.used += 1
        made = pltpu.make_async_remote_copy(
            src_ref=src,
            dst_ref=dst,
            send_sem=self.send.at[i],
            recv_sem=self.recv.at[i],
            device_id=where,
            device_id_type=MESH,
        )
        self.all.append(made)
        return made


def start(copies):
    for made in copies:
        made.start()


def arrived(copies):
    for made in copies:
        made.wait_recv()


class Gather:
    def __init__(self, comm, buf, x_first):
        self.buf, self.x_first = buf, x_first
        self.rows = buf.shape[2]
        i, j = (comm.y, comm.x) if x_first else (comm.x, comm.y)
        near, far = (comm.at_x, comm.at_y) if x_first else (comm.at_y, comm.at_x)
        h = self.rows // 2
        jl, jr = lax.rem(j + 3, 4), lax.rem(j + 1, 4)
        il, ir = lax.rem(i + 3, 4), lax.rem(i + 1, 4)
        low, high = pl.ds(0, h), pl.ds(h, h)
        b = self.block
        self.steps = [
            [comm.copy(b(i, j), b(i, j), near(1)), comm.copy(b(i, j), b(i, j), near(3))],
            [
                comm.copy(b(i, jl, low), b(i, jl, low), near(1)),
                comm.copy(b(i, jr, high), b(i, jr, high), near(3)),
            ],
            [
                comm.copy(b(i, pl.ds(0, 4)), b(i, pl.ds(0, 4)), far(1)),
                comm.copy(b(i, pl.ds(0, 4)), b(i, pl.ds(0, 4)), far(3)),
            ],
            [
                comm.copy(b(il, pl.ds(0, 2)), b(il, pl.ds(0, 2)), far(1)),
                comm.copy(b(ir, pl.ds(2, 2)), b(ir, pl.ds(2, 2)), far(3)),
            ],
        ]

    def block(self, i, j, rows=None):
        index = (i, j) if self.x_first else (j, i)
        return self.buf.at[index] if rows is None else self.buf.at[index + (rows,)]


class Scatter:
    def __init__(self, comm, buf, y_first, r1, r2, r3, r4):
        self.buf, self.y_first = buf, y_first
        self.rows = buf.shape[2]
        i, j = (comm.y, comm.x) if y_first else (comm.x, comm.y)
        first, second = (comm.at_y, comm.at_x) if y_first else (comm.at_x, comm.at_y)
        self.i, self.j = i, j
        self.r = (r1, r2, r3, r4)
        h = self.rows // 2
        self.i1, self.i2, self.i3 = (lax.rem(i + k, 4) for k in (1, 2, 3))
        self.j1, self.j2, self.j3 = (lax.rem(j + k, 4) for k in (1, 2, 3))
        b = self.block
        self.s1 = [
            comm.copy(b(self.i2, pl.ds(0, 2)), r1.at[0], first(1)),
            comm.copy(b(self.i2, pl.ds(2, 2)), r1.at[1], first(3)),
        ]
        self.s2 = [
            comm.copy(b(self.i1, pl.ds(0, 4)), r2.at[0], first(1)),
            comm.copy(b(self.i3, pl.ds(0, 4)), r2.at[1], first(3)),
        ]
        self.s3 = [
            comm.copy(b(i, self.j2, pl.ds(0, h)), r3.at[0], second(1)),
            comm.copy(b(i, self.j2, pl.ds(h, h)), r3.at[1], second(3)),
        ]
        self.s4 = [
            comm.copy(b(i, self.j1), r4.at[0], second(1)),
            comm.copy(b(i, self.j3), r4.at[1], second(3)),
        ]

    def index(self, i, j):
        return (i, j) if self.y_first else (j, i)

    def block(self, i, j, rows=None):
        index = self.index(i, j)
        return self.buf.at[index] if rows is None else self.buf.at[index + (rows,)]

    def add(self, index, *others):
        total = self.buf[index].astype(F32)
        for other in others:
            total = total + other.astype(F32)
        self.buf[index] = total.astype(BF16)

    def step1(self):
        start(self.s1)

    def step2(self):
        arrived(self.s1)
        r1 = self.r[0]

        def body(k, _):
            self.add(self.index(self.i1, k), r1[0, k])
            self.add(self.index(self.i3, k + 2), r1[1, k])
            return 0

        lax.fori_loop(0, 2, body, 0)
        start(self.s2)

    def step3(self):
        arrived(self.s2)
        r2 = self.r[1]

        def body(k, _):
            self.add(self.index(self.i, k), r2[0, k], r2[1, k])
            return 0

        lax.fori_loop(0, 4, body, 0)
        start(self.s3)

    def step4(self):
        arrived(self.s3)
        r3 = self.r[2]
        h = self.rows // 2
        self.add(self.index(self.i, self.j1) + (pl.ds(0, h),), r3[0])
        self.add(self.index(self.i, self.j3) + (pl.ds(h, h),), r3[1])
        start(self.s4)

    def finish(self):
        arrived(self.s4)
        r4 = self.r[3]
        own = self.buf[self.index(self.i, self.j)].astype(F32)
        return own + r4[0].astype(F32) + r4[1].astype(F32)


def kernel(
    q_in, k_ref, v_ref, g_in, x_in, gy_in, ids_ref, rw_ref, w_in, wd_in, sink_ref, freq_ref,
    out_hbm, dq_hbm, dk_ref, dv_ref, ds_ref, z_hbm, share_ref, one_ref, dw_hbm, dwd_hbm,
    out_ref, dq_ref, x_ref, gy_ref, w3, wd_ref, wi,
    kb, vb, xb, yb, zs, zr, zs2, zr2, qz, qzt, gz, gzt, kk, vv, kt, vt, e_s, dp_s, m_s, st, ot, dqt,
    dka0, dka1, dva0, dva1, dkp, dvp, wg, wu, hid, dgu, py, px,
    ry1, ry2, ry3, ry4, rx1, rx2, rx3, rx4, k01, k02, k03, k04, k11, k12, k13, k14, v01, v02, v03, v04, v11, v12, v13, v14,
    rw, rwd, sx, sy, sz, sc,
    send, recv, local,
):
    cm = Comm(send, recv)
    me = cm.y * 4 + cm.x

    barrier = pltpu.get_barrier_semaphore()
    partners = [cm.at_x(k) for k in (1, 2, 3)] + [cm.at_y(k) for k in (1, 2, 3)]
    partners += [cm.at_z(k) for k in range(1, 8)] + [cm.at_c()]
    for where in partners:
        pl.semaphore_signal(barrier, inc=1, device_id=where, device_id_type=MESH)

    pairs = ((x_in, x_ref), (gy_in, gy_ref), (q_in, out_ref), (g_in, dq_ref), (w_in, w3), (wd_in, wd_ref))
    loads = [pltpu.make_async_copy(a, b, local.at[i]) for i, (a, b) in enumerate(pairs)]
    for load in loads:
        load.start()
    pairs = (
        (out_ref, out_hbm), (dq_ref, dq_hbm), (zr2, z_hbm), (w3, dw_hbm), (wd_ref, dwd_hbm),
    )
    stores = [pltpu.make_async_copy(a, b, local.at[6 + i]) for i, (a, b) in enumerate(pairs)]
    out_store, dq_store, z_store, dw_store, dwd_store = stores

    g_k, g_v = Gather(cm, kb, True), Gather(cm, vb, False)
    g_x, g_y = Gather(cm, xb, True), Gather(cm, yb, False)
    z_out = [
        cm.copy(zs.at[lax.rem(cm.z + k, 8)], zr.at[cm.z], cm.at_z(k)) for k in range(1, 8)
    ]
    z_back = [
        cm.copy(zs2.at[lax.rem(cm.z + k, 8)], zr2.at[cm.z], cm.at_z(k)) for k in range(1, 8)
    ]
    s_kv = [
        (Scatter(cm, dka0, True, k01, k02, k03, k04), Scatter(cm, dva0, False, v01, v02, v03, v04)),
        (Scatter(cm, dka1, True, k11, k12, k13, k14), Scatter(cm, dva1, False, v11, v12, v13, v14)),
    ]
    s_y, s_x = Scatter(cm, py, True, ry1, ry2, ry3, ry4), Scatter(cm, px, False, rx1, rx2, rx3, rx4)
    dw_out = [cm.copy(wi, rw, cm.at_c()), cm.copy(wg, rwd, cm.at_c())]
    sink_x = [cm.copy(sx.at[cm.x], sx.at[cm.x], cm.at_x(k)) for k in (1, 2, 3)]
    sink_y = [cm.copy(sy.at[cm.y], sy.at[cm.y], cm.at_y(k)) for k in (1, 2, 3)]
    sink_z = [cm.copy(sz.at[cm.z], sz.at[cm.z], cm.at_z(k)) for k in range(1, 8)]
    sink_c = [cm.copy(sc.at[cm.c], sc.at[cm.c], cm.at_c())]

    lanes = lax.broadcasted_iota(jnp.int32, (128, 128), 1)
    subs = lax.broadcasted_iota(jnp.int32, (128, 128), 0)
    angles = (subs + me * 128).astype(F32) * freq_ref[...]
    cos_t = jnp.cos(angles) * CONCENTRATION
    sin_t = jnp.sin(angles) * jnp.where((lanes & 32) == 0, -CONCENTRATION, CONCENTRATION)

    for t in range(2):
        part = k_ref[:, t * 128 : (t + 1) * 128].astype(F32)
        kb[cm.y, cm.x, :, t * 128 : (t + 1) * 128] = (
            part * cos_t + swap_halves(part, lanes) * sin_t
        ).astype(BF16)
    vb[cm.y, cm.x] = v_ref[...]

    expert, place = subs >> 4, subs & 7
    hit = jnp.zeros((128, 128), F32)
    share = jnp.zeros((128, 128), F32)
    for k in range(TOP):
        match = ids_ref[k : k + 1, :] == expert
        hit = jnp.where(match, 1.0, hit)
        share = share + jnp.where(match, rw_ref[k : k + 1, :], 0.0)
    upper = jnp.where(subs <= lanes, 1.0, 0.0).astype(BF16)
    rank = jnp.where(hit > 0.5, dot(hit.astype(BF16), upper), 0.0).astype(jnp.int32)
    pick_x = (rank == place + 1) & (place < CAP)
    pick_y = (rank == place - CAP + 1) & (place >= CAP)
    one_x = jnp.where(pick_x, 1.0, 0.0)
    one_y = jnp.where(pick_y, 1.0, 0.0)
    share_y = jnp.sum(jnp.where(pick_y, share, 0.0), axis=1, keepdims=True)
    share_ref[...] = jnp.where(pick_x, share, 0.0)
    one_ref[...] = one_y
    is_low = (subs & 8) == 0

    def parts(table):
        low = jnp.where(is_low, table, 0.0)
        return low.astype(BF16), (table - low).astype(BF16)

    pl.semaphore_wait(barrier, len(partners))
    start(g_k.steps[0] + g_v.steps[0])

    for load in loads[:2]:
        load.wait()
    (x_low, x_high), (y_low, y_high) = parts(one_x), parts(one_y)
    picked = dot(x_low, x_ref[:PIECE], NT) + dot(x_high, x_ref[CUT:], NT)
    picked += (dot(y_low, gy_ref[:PIECE], NT) + dot(y_high, gy_ref[CUT:], NT)) * share_y
    zs[...] = picked.astype(BF16).reshape(8, 16, PIECE)
    start(z_out)
    zr[cm.z] = zs[cm.z]

    def prepare(t, _):
        cut = pl.ds(pl.multiple_of(t * 128, 128), 128)
        part = out_ref[:, cut].astype(F32)
        part = (part * cos_t + swap_halves(part, lanes) * sin_t).astype(BF16).astype(F32)
        part = part * SCORE_SCALE
        grad = dq_ref[:, cut].astype(F32)
        for p in range(2):
            rows = slice(p * 128, (p + 1) * 128)
            one = jnp.where((lanes >> 6) == p, part, 0.0)
            qz[t, rows, :] = one.astype(BF16)
            qzt[t, :, rows] = one.T.astype(BF16)
            one = jnp.where((lanes >> 6) == p, grad, 0.0)
            gz[t, rows, :] = one.astype(BF16)
            gzt[t, :, rows] = one.T.astype(BF16)
        return 0

    arrived(g_k.steps[0] + g_v.steps[0])
    start(g_k.steps[1] + g_v.steps[1])
    for load in loads[2:4]:
        load.wait()
    lax.fori_loop(0, 5, prepare, 0)
    arrived(g_k.steps[1] + g_v.steps[1])
    start(g_k.steps[2] + g_v.steps[2])
    lax.fori_loop(5, 16, prepare, 0)
    arrived(g_k.steps[2] + g_v.steps[2])
    start(g_k.steps[3] + g_v.steps[3])

    arrived(z_out)
    r_i = lax.broadcasted_iota(jnp.int32, (ROWS, 128), 0)
    c_i = lax.broadcasted_iota(jnp.int32, (ROWS, 128), 1)
    home = (r_i >> 2) * 16 + (r_i & 3)
    takes = [jnp.where(c_i == home + k, 1.0, 0.0).astype(BF16) for k in (0, 4, 8, 12)]
    landed = zr[...].reshape(128, PIECE)
    for own, low, high in ((xb, takes[0], takes[2]), (yb, takes[1], takes[3])):
        own[cm.y, cm.x] = jnp.concatenate(
            [dot(low, landed[:, :CUT]).astype(BF16), dot(high, landed).astype(BF16)], axis=1
        )

    start(g_x.steps[0] + g_y.steps[0])

    for load in loads[4:]:
        load.wait()
    wi[...] = w3[...].reshape(2 * FFD, D)
    r_i = lax.broadcasted_iota(jnp.int32, (FFD, 2 * FFD), 0)
    c_i = lax.broadcasted_iota(jnp.int32, (FFD, 2 * FFD), 1)
    spread_g = jnp.where(c_i == 2 * r_i, 1.0, 0.0).astype(BF16)
    spread_u = jnp.where(c_i == 2 * r_i + 1, 1.0, 0.0).astype(BF16)
    wg[...] = dot(spread_g, wi[...]).astype(BF16)
    wu[...] = dot(spread_u, wi[...]).astype(BF16)

    def clear(k, _):
        for total in (dka0, dka1, dva0, dva1):
            total[k // 4, lax.rem(k, 4)] = jnp.zeros((128, 128), BF16)
        return 0

    lax.fori_loop(0, 16, clear, 0)
    arrived(g_k.steps[3] + g_v.steps[3])

    wide = me // 4 + 1
    key_in = lax.broadcasted_iota(jnp.int32, (512, 512), 0)
    query_in = lax.rem(lax.broadcasted_iota(jnp.int32, (512, 512), 1), 128)
    lanes2 = lax.broadcasted_iota(jnp.int32, (512, 128), 1)

    def lane_cut(group):
        return pl.ds(pl.multiple_of((group // 2) * 128, 128), 128), lax.rem(group, 2)

    def spread_keys(group):
        cut, odd = lane_cut(group)

        def spread(j, _):
            for source, twice, turned in ((kb, kk, kt), (vb, vv, vt)):
                part = source[j, :, :, cut].reshape(512, 128).astype(F32)
                part = jnp.where((lanes2 >> 6) == odd, part, 0.0)
                part = part + pltpu.roll(part, 64, 1)
                twice[j] = part.astype(BF16)
                turned[j] = part.T[:64].astype(BF16)
            dkp[j] = jnp.zeros((512, 128), F32)
            dvp[j] = jnp.zeros((512, 128), F32)
            return 0

        lax.fori_loop(0, wide, spread, 0)

    def collect_keys(group, half):
        odd = lax.rem(group, 2)
        totals = ((dkp, (dka0, dka1)[half]), (dvp, (dva0, dva1)[half]))

        def collect(j, _):
            for source, total in totals:
                part = source[j]
                part = part + pltpu.roll(part, 64, 1)
                part = jnp.where((lanes2 >> 6) == odd, part, 0.0)
                old = total[j].reshape(512, 128).astype(F32)
                total[j] = (old + part).astype(BF16).reshape(4, 128, 128)
            return 0

        lax.fori_loop(0, wide, collect, 0)

    def scores(hh):
        t0, t1 = 2 * hh, 2 * hh + 1
        sink_row = jnp.concatenate(
            [jnp.full((1, 128), sink_ref[4 * hh + b], F32) for b in range(4)], axis=1
        )

        def first(j, carry, masked):
            top, z_sum, d_sum = carry
            keys = kk[j]
            s = jnp.concatenate([dot(keys, qzt[t0]), dot(keys, qzt[t1])], axis=1)
            if masked:
                s = jnp.where(key_in + (j * 512 - me * 128) <= query_in, s, -1e30)
            new_top = jnp.maximum(top, jnp.max(s, axis=0, keepdims=True))
            keep = jnp.exp(top - new_top)
            e = jnp.exp(s - new_top)
            vals = vv[j]
            dp = jnp.concatenate([dot(vals, gzt[t0]), dot(vals, gzt[t1])], axis=1)
            e_s[j] = e
            dp_s[j] = dp
            m_s[j] = jnp.broadcast_to(new_top, (8, 512))
            z_sum = z_sum * keep + jnp.sum(e, axis=0, keepdims=True)
            d_sum = d_sum * keep + jnp.sum(e * dp, axis=0, keepdims=True)
            return new_top, z_sum, d_sum

        carry = (sink_row, jnp.ones((1, 512), F32), jnp.zeros((1, 512), F32))
        carry = lax.fori_loop(0, wide - 1, lambda j, c: first(j, c, False), carry)
        top, z_sum, d_sum = first(wide - 1, carry, True)
        inv = 1.0 / z_sum
        delta = d_sum * inv
        sx[cm.x, pl.ds(hh, 1), :] = -jnp.exp(sink_row - top) * inv * delta
        for k, row in enumerate((top, inv, delta)):
            st[k] = jnp.broadcast_to(row, (8, 512))

    def gradients(hh):
        t0 = 2 * hh
        top, inv, delta = (st[k][0:1] for k in range(3))
        ot[...] = jnp.zeros((64, 512), F32)
        dqt[...] = jnp.zeros((64, 512), F32)

        def second(j, _):
            scale = jnp.exp(m_s[j][0:1] - top) * inv
            p = e_s[j] * scale
            pb = p.astype(BF16)
            ds = (p * (dp_s[j] - delta)).astype(BF16)
            dvp[j] += dot(pb, gz[pl.ds(t0, 2)].reshape(512, 128))
            dkp[j] += dot(ds, qz[pl.ds(t0, 2)].reshape(512, 128))
            ot[...] += dot(vt[j], pb)
            dqt[...] += dot(kt[j], ds)
            return 0

        lax.fori_loop(0, wide, second, 0)

        for i in range(2):
            cut = pl.ds(pl.multiple_of((2 * hh + i) * 128, 128), 128)
            lo, hi = slice(i * 256, i * 256 + 128), slice(i * 256 + 128, i * 256 + 256)
            out_ref[:, cut] = jnp.concatenate([ot[:, lo], ot[:, hi]], axis=0).T.astype(BF16)
            back = jnp.concatenate([dqt[:, lo], dqt[:, hi]], axis=0).T * SCORE_SCALE
            dq_ref[:, cut] = (back * cos_t - swap_halves(back, lanes) * sin_t).astype(BF16)

    def attend(u, half, hooks):
        hh = u // 2
        pl.when(lax.rem(u, 4) == 0)(lambda: spread_keys(hh // 2))
        pl.when(lax.rem(u, 2) == 0)(lambda: scores(hh))
        pl.when(lax.rem(u, 2) == 1)(lambda: gradients(hh))
        pl.when(lax.rem(u, 4) == 3)(lambda: collect_keys(hh // 2, half))
        for when, hook in hooks:
            pl.when(u == when)(hook)
        return 0

    def gather_on(step):
        def hook():
            arrived(g_x.steps[step] + g_y.steps[step])
            start(g_x.steps[step + 1] + g_y.steps[step + 1])

        return hook

    gather_on(0)()
    hooks = ((0, gather_on(1)), (5, gather_on(2)))
    lax.fori_loop(0, 8, lambda u, _: attend(u, 0, hooks), 0)

    def kv_on(half, name):
        getattr(s_kv[half][0], name)()
        getattr(s_kv[half][1], name)()

    kv_on(0, "step1")

    arrived(g_x.steps[3] + g_y.steps[3])

    def expert_rows(k, _):
        rows = xb[pl.ds(2 * k, 2)].reshape(256, D)
        grads = yb[pl.ds(2 * k, 2)].reshape(256, D)
        gate = dot(rows, wg[...], NT)
        up = dot(rows, wu[...], NT)
        dh = dot(grads, wd_ref[...], NT)
        sig = 1.0 / (1.0 + jnp.exp(-SWIGLU_ALPHA * gate))
        lift = sig * (up + 1.0)
        hid[pl.ds(2 * k, 2)] = (gate * lift).astype(BF16).reshape(2, 4, ROWS, FFD)
        dg = dh * lift * (1.0 + SWIGLU_ALPHA * gate * (1.0 - sig))
        du = dh * gate * sig
        both = dot(dg.astype(BF16), spread_g) + dot(du.astype(BF16), spread_u)
        dgu[pl.ds(2 * k, 2)] = both.astype(BF16).reshape(2, 4, ROWS, 2 * FFD)
        return 0

    lax.fori_loop(0, 2, expert_rows, 0)

    def y_rows(i):
        py[i] = dot(hid[i].reshape(128, FFD), wd_ref[...]).astype(BF16).reshape(4, ROWS, D)

    def x_rows(i):
        px[:, i] = dot(dgu[:, i].reshape(128, 2 * FFD), wi[...]).astype(BF16).reshape(4, ROWS, D)

    def chunk(k, _):
        y_rows(lax.rem(cm.y + k, 4))
        x_rows(lax.rem(cm.x + k, 4))
        return 0

    kv_on(0, "step2")
    chunk(2, 0)
    s_y.step1()
    s_x.step1()
    lax.fori_loop(0, 2, lambda k, _: chunk(2 * k + 1, 0), 0)
    chunk(0, 0)

    turned = dgu[...].reshape(512, 2 * FFD).astype(F32).T.astype(BF16)
    turned_h = hid[...].reshape(512, FFD).astype(F32).T.astype(BF16)
    for lo in range(0, D, 512):
        cut = slice(lo, min(lo + 512, D))
        wi[:, cut] = dot(turned, xb[:, :, :, cut].reshape(512, -1)).astype(BF16)
        wg[:, cut] = dot(turned_h, yb[:, :, :, cut].reshape(512, -1)).astype(BF16)
    start(dw_out)
    kv_on(0, "step3")

    def both_sums(name):
        def hook():
            getattr(s_y, name)()
            getattr(s_x, name)()

        return hook

    def send_back():
        y_own = s_y.finish().astype(BF16)
        x_own = s_x.finish().astype(BF16)
        returned = dot(takes[0], y_own[:, :PIECE], TN) + dot(takes[1], x_own[:, :PIECE], TN)
        returned += dot(takes[2], y_own[:, CUT:], TN) + dot(takes[3], x_own[:, CUT:], TN)
        zs2[...] = returned.astype(BF16).reshape(8, 16, PIECE)
        start(z_back)
        zr2[cm.z] = zs2[cm.z]

    hooks = (
        (8, both_sums("step2")), (8, lambda: kv_on(0, "step4")), (13, both_sums("step3")), (14, both_sums("step4")),
        (14, lambda: start(sink_x)),
    )
    lax.fori_loop(8, 16, lambda u, _: attend(u, 1, hooks), 0)

    kv_on(1, "step1")
    send_back()
    out_store.start()
    dq_store.start()
    arrived(sink_x)
    sy[cm.y] = ((sx[0] + sx[1]) + sx[2]) + sx[3]
    start(sink_y)
    kv_on(1, "step2")
    arrived(sink_y)
    sz[cm.z] = ((sy[0] + sy[1]) + sy[2]) + sy[3]
    start(sink_z)

    arrived(dw_out)
    for lo in range(0, D, 512):
        cut = slice(lo, min(lo + 512, D))
        total = wi[:, cut].astype(F32) + rw[:, cut].astype(F32)
        w3[:, :, cut] = total.astype(BF16).reshape(FFD, 2, -1)
        wd_ref[:, cut] = (wg[:, cut].astype(F32) + rwd[:, cut].astype(F32)).astype(BF16)
    dw_store.start()
    dwd_store.start()

    kv_on(1, "step3")
    arrived(sink_z)
    total = sz[0]
    for k in range(1, 8):
        total = total + sz[k]
    sc[cm.c] = total
    start(sink_c)
    kv_on(1, "step4")

    for t, (k_part, v_part) in enumerate(s_kv):
        cut = slice(t * 128, (t + 1) * 128)
        part = k_part.finish()
        dk_ref[:, cut] = (part * cos_t - swap_halves(part, lanes) * sin_t).astype(BF16)
        dv_ref[:, cut] = v_part.finish().astype(BF16)

    arrived(sink_c)
    total = sc[0] + sc[1]
    row8 = lax.broadcasted_iota(jnp.int32, (8, HQ), 0)
    lane8 = lax.broadcasted_iota(jnp.int32, (8, HQ), 1)
    sums = jnp.zeros((8, HQ), F32)
    for b in range(4):
        part = jnp.sum(total[:, b * 128 : (b + 1) * 128], axis=1, keepdims=True)
        sums = sums + jnp.where(lane8 == 4 * row8 + b, part, 0.0)
    ds_ref[...] = jnp.sum(sums, axis=0, keepdims=True)

    arrived(z_back)
    z_store.start()
    for made in cm.all:
        made.wait_send()
    for store in stores:
        store.wait()


def finish(*refs):
    (z_ref, share_ref, one_ref), refs = refs[:3], refs[3:]
    sources, (moe_hbm, dx_hbm), results, held = refs[:7], refs[7:9], refs[9:16], refs[16:23]
    moe, dx, sems = refs[23:]
    loads = [pltpu.make_async_copy(sources[i], held[i], sems.at[i]) for i in range(7)]
    stores = [pltpu.make_async_copy(held[i], results[i], sems.at[7 + i]) for i in range(7)]
    last = [
        pltpu.make_async_copy(made.at[cut], place.at[cut], sems.at[14 + 2 * i + j])
        for i, cut in enumerate((pl.ds(0, CUT), pl.ds(CUT, D - CUT)))
        for j, (made, place) in enumerate(((moe, moe_hbm), (dx, dx_hbm)))
    ]
    for load in loads:
        load.start()

    low_rows = (lax.broadcasted_iota(jnp.int32, (128, 128), 0) & 8) == 0
    share = share_ref[...]
    top = share.astype(BF16).astype(F32)
    tables = []
    for table in (top, share - top, one_ref[...]):
        low = jnp.where(low_rows, table, 0.0)
        tables.append((low.astype(BF16), (table - low).astype(BF16)))
    where = ((0, 768, 0, 0), (768, 640, 768, 0), (0, 768, CUT, 1), (768, 704, CUT + 768, 1))
    for load, store in zip(loads, stores):
        load.wait()
        store.start()
    for i, (lane, n, at, high) in enumerate(where):
        back = z_ref[:, :, lane : lane + n].reshape(128, n)
        moe[at : at + n] = (dot(back, tables[0][high], TN) + dot(back, tables[1][high], TN)).astype(BF16)
        dx[at : at + n] = dot(back, tables[2][high], TN).astype(BF16)
        if i % 2 == 1:
            for made in last[i - 1 : i + 1]:
                made.start()
    for made in stores + last:
        made.wait()


def frequencies():
    steps_f = np.arange(HD // 2, dtype=np.float32)
    extrap_freq = np.float32(1.0) / np.exp(steps_f * np.float32(2.0 * math.log(ROPE_BASE) / HD))
    interp_freq = extrap_freq / np.float32(YARN_FACTOR)
    low_end = HD * math.log(YARN_INITIAL / (BETA_FAST * 2.0 * math.pi)) / (2.0 * math.log(ROPE_BASE))
    high_end = HD * math.log(YARN_INITIAL / (BETA_SLOW * 2.0 * math.pi)) / (2.0 * math.log(ROPE_BASE))
    ramp_val = np.clip((steps_f - np.float32(low_end)) / np.float32(high_end - low_end), 0.0, 1.0)
    inv_freq = interp_freq * ramp_val + extrap_freq * (np.float32(1.0) - ramp_val)
    return jnp.asarray(np.tile(inv_freq, 4)[None, :], F32)


def body(query, keys, values, sinks, attn_grad, moe_in, moe_grad, expert_ids, route_weights, w_gate_up, w_down):
    rows = query.shape[1]
    vmem = pl.BlockSpec(memory_space=pltpu.VMEM)

    def v(*shape, dtype=BF16):
        return pltpu.VMEM(shape, dtype)

    def sums(r, c):
        return [v(2, 2, r, c), v(2, 4, r, c), v(2, r // 2, c), v(2, r, c)]

    scratch = [
        v(rows, HQ * HD), v(rows, HQ * HD), v(D, rows), v(D, rows), v(FFD, 2, D), v(FFD, D), v(2 * FFD, D),
        v(4, 4, 128, 256), v(4, 4, 128, 256), v(4, 4, ROWS, D), v(4, 4, ROWS, D),
        v(8, 16, PIECE), v(8, 16, PIECE), v(8, 16, PIECE), v(8, 16, PIECE),
        v(16, 256, 128), v(16, 128, 256), v(16, 256, 128), v(16, 128, 256),
        v(4, 512, 128), v(4, 512, 128), v(4, 64, 512), v(4, 64, 512),
        v(4, 512, 512, dtype=F32), v(4, 512, 512, dtype=F32), v(4, 8, 512, dtype=F32),
        v(3, 8, 512, dtype=F32), v(64, 512, dtype=F32), v(64, 512, dtype=F32),
        *[v(4, 4, 128, 128)] * 4, v(4, 512, 128, dtype=F32), v(4, 512, 128, dtype=F32),
        v(FFD, D), v(FFD, D), v(4, 4, ROWS, FFD), v(4, 4, ROWS, 2 * FFD),
        v(4, 4, ROWS, D), v(4, 4, ROWS, D),
        *sums(ROWS, D), *sums(ROWS, D), *sums(128, 128) * 4,
        v(2 * FFD, D), v(FFD, D),
        v(4, 8, 512, dtype=F32), v(4, 8, 512, dtype=F32), v(8, 8, 512, dtype=F32), v(2, 8, 512, dtype=F32),
        pltpu.SemaphoreType.DMA((112,)),
        pltpu.SemaphoreType.DMA((112,)),
        pltpu.SemaphoreType.DMA((12,)),
    ]
    sds = jax.ShapeDtypeStruct
    attn = [
        sds((rows, HQ * HD), BF16), sds((rows, HQ * HD), BF16),
        sds((rows, HK * HD), BF16), sds((rows, HK * HD), BF16), sds((1, HQ), F32),
    ]
    weights = [sds((FFD, 2, D), BF16), sds((FFD, D), BF16)]
    back = [sds((8, 16, PIECE), BF16)] + [sds((128, rows), F32)] * 2
    token = [sds((D, rows), BF16)] * 2
    hbm = pl.BlockSpec(memory_space=pl.ANY)
    smem = pl.BlockSpec(memory_space=pltpu.SMEM)
    outs = pl.pallas_call(
        kernel,
        out_shape=attn + back + weights,
        in_specs=[hbm, vmem, vmem, hbm, hbm, hbm, vmem, vmem, hbm, hbm, smem, vmem],
        out_specs=[hbm, hbm, vmem, vmem, vmem, hbm, vmem, vmem, hbm, hbm],
        scratch_shapes=scratch,
        compiler_params=pltpu.CompilerParams(
            collective_id=0, has_side_effects=True, vmem_limit_bytes=63 * 1024 * 1024
        ),
        name="layer",
    )(
        query[0], keys[0], values[0], attn_grad[0], moe_in[0].T, moe_grad[0].T,
        expert_ids[0].T, route_weights[0].T,
        jnp.transpose(w_gate_up[0], (2, 1, 0)), w_down[0], sinks, frequencies(),
    )
    outs = pl.pallas_call(
        finish,
        out_shape=token + attn + weights,
        in_specs=[vmem] * 3 + [hbm] * 7,
        out_specs=[hbm] * 9,
        scratch_shapes=[v(*one.shape, dtype=one.dtype) for one in attn + weights + token]
        + [pltpu.SemaphoreType.DMA((18,))],
        compiler_params=pltpu.CompilerParams(vmem_limit_bytes=63 * 1024 * 1024),
        name="finish",
    )(*outs[5:8], *outs[:5], *outs[8:])
    moe_out, d_moe_in, attn_out, d_query, d_keys, d_values, d_sinks, d_gate_up, d_down = outs
    return (
        attn_out[None], d_query[None], d_keys[None], d_values[None], d_sinks.reshape(HQ),
        moe_out.T[None], d_moe_in.T[None], jnp.transpose(d_gate_up, (2, 1, 0))[None], d_down[None],
    )


def solution(mesh):
    rows = P(("dp", "exp"), "seq", None)
    gate_up, down = P("exp", None, None, "seq"), P("exp", "seq", None)
    return jax.shard_map(
        body,
        mesh=mesh,
        in_specs=(rows, rows, rows, P(), rows, rows, rows, rows, rows, gate_up, down),
        out_specs=(rows, rows, rows, rows, P(), rows, rows, gate_up, down),
        check_vma=False,
    )
```
